512 devices in a mesh: rx: 32 (over z_lo, x), tx: 16 (over y, z_hi, core).
Axes of the slice: x: 4, y: 4, z: 16 (z_hi: 2, z_lo: 8; z = z_hi * 8 + z_lo), core: 2. Of those that a mesh axis runs over, the one named last changes fastest.
Arguments:
- sender_xy: int32 [2, 32768], P(None, ('tx', 'rx')), may hold values from 0 to 255, as said below
- listener_xy: int32 [2, 32768], P(None, ('rx', 'tx')), may hold values from 0 to 256, as said below
- powers: float32 [32768, 128], P(('tx', 'rx')), may hold values from 0.25 to 1
- weight: int32 [32768], P(('rx', 'tx')), may hold values from 1 to 16
- fairness: int32 [32768], P(('rx', 'tx')), may hold values from 0 to 2
- step_code: int32 [1], replicated, may hold values from 256 to 4096
Outputs:
- quality: float32 [32768, 128], P(('rx', 'tx'))
- gradient: float32 [32768, 128], P(('tx', 'rx'))
- new_power: float32 [32768, 128], P(('tx', 'rx'))
- duality_gap: float32 [1], replicated
The draws below stay inside these ranges and needn't reach their ends.
Inputs may be any that keep to these rules, and one draw needn't show every extreme that they name: `sender_xy`: row 0 lies in 0 to 255 and row 1 in 0 to 255. `listener_xy`: each entry equals the sender_xy entry of the same user or exceeds it by one.
All inputs are finite; a program needn't handle non-finite values.
Results may differ from the reference program's by a relative error of at most 0.0003.
Values sent between devices are 32-bit elements; how exact they have to be, the bound alone decides.
No kernel may reach another device: no remote copies, remote signals or barrier semaphores. Data moves between devices by JAX's collectives and lax.ppermute only.
A program may use at most 64 MiB of HBM per device.

```python
import math
import jax
import jax.numpy as jnp
from jax import lax

CHANNELS = 128
SIDE = 256
USERS = 32768
LENGTH_Y = 256


def place_users(key):
    base = jax.random.fold_in(key, 11)
    key_across, key_length, key_shift = jax.random.split(base, 3)
    across = jax.random.randint(key_across, (USERS,), 0, SIDE, dtype=jnp.int32).at[0].set(SIDE - 1)
    lengthwise = jax.random.randint(key_length, (USERS,), 0, LENGTH_Y, dtype=jnp.int32).at[0].set(LENGTH_Y - 1)
    shifts = jax.random.randint(key_shift, (2, USERS), 0, 2, dtype=jnp.int32).at[:, 0].set(1)
    sender = jnp.stack([across, lengthwise])
    return (sender, sender + shifts)


def draw_sender_xy(key, part):
    return place_users(key)[0]


def draw_listener_xy(key, part):
    return place_users(key)[1]


def set_ends(result, rng, smallest, top_value):
    longest = result.shape.index(max(result.shape))
    spots = []
    for shift in (0, 1):
        where = [jax.random.randint(jax.random.fold_in(rng, axis), (), 0, length) for axis, length in enumerate(result.shape)]
        where[longest] = (where[longest] + shift) % result.shape[longest]
        spots.append(tuple(where))
    return result.at[spots[0]].set(smallest).at[spots[1]].set(top_value)


def level_of(stream_key, shape, cuts, smallest, largest):
    factor_of = 1.0
    for position, blocks in cuts:
        draws = jax.random.uniform(jax.random.fold_in(jax.random.fold_in(stream_key, 6), position), (blocks,), jnp.float32, smallest / len(cuts), largest / len(cuts))
        factor_of = factor_of * jnp.repeat(jnp.exp(draws), shape[position] // blocks).reshape((-1,) + (1,) * (len(shape) - 1 - position))
    return factor_of


def setup_inputs(seed: int = 0) -> dict:
    seeds = jax.random.split(jax.random.key(seed), 7)
    sender_xy = draw_sender_xy(jax.random.fold_in(seeds[6], 71), 0)
    listener_xy = draw_listener_xy(jax.random.fold_in(seeds[6], 71), 0)
    powers = jnp.clip(jnp.exp(math.log(1.0) - 1.3862944 * jax.random.uniform(seeds[2], (USERS, CHANNELS), jnp.float32) ** level_of(seeds[2], (USERS, CHANNELS), ((0, 512),), -0.2, 0.2)), 0.25, 1.0)
    weight = set_ends(jax.random.randint(seeds[3], (USERS,), 1, 17), jax.random.fold_in(seeds[3], 1), 1, 16).astype(jnp.int32)
    fairness = set_ends(jax.random.randint(seeds[4], (USERS,), 0, 3), jax.random.fold_in(seeds[4], 1), 0, 2).astype(jnp.int32)
    step_code = jax.random.randint(seeds[5], (1,), 256, 4097).astype(jnp.int32)
    return dict(sender_xy=sender_xy, listener_xy=listener_xy, powers=powers, weight=weight, fairness=fairness, step_code=step_code)


NOISE_POWER = 0.05
ARRAY_GAIN = 32.0
WEIGHT_UNIT = 1.0 / 16.0
PEAK_POWER = 1.0


def path_gain(listen, sender):
    delta_x = listen[0].astype(jnp.float32)[:, None] - sender[0].astype(jnp.float32)[None, :]
    delta_y = listen[1].astype(jnp.float32)[:, None] - sender[1].astype(jnp.float32)[None, :]
    return 1.0 / (1.0 + delta_x * delta_x + delta_y * delta_y)


def reference(sender_xy, listener_xy, powers, weight, fairness, step_code):
    block_rows = min(512, USERS)
    blocks = USERS // block_rows
    own_x = listener_xy[0].astype(jnp.float32) - sender_xy[0].astype(jnp.float32)
    own_y = listener_xy[1].astype(jnp.float32) - sender_xy[1].astype(jnp.float32)
    own_gain = 1.0 / (1.0 + own_x * own_x + own_y * own_y)
    listen_blocks = listener_xy.reshape(2, blocks, block_rows).transpose(1, 0, 2)
    starts = jnp.arange(blocks, dtype=jnp.int32) * block_rows
    columns = jnp.arange(USERS, dtype=jnp.int32)

    def crossing(listen, first_row):
        gain_tile = path_gain(listen, sender_xy)
        row_ids = first_row + jnp.arange(block_rows, dtype=jnp.int32)
        return jnp.where(row_ids[:, None] == columns[None, :], 0.0, gain_tile)

    def row_pass(inputs):
        listen, first_row = inputs
        return jnp.dot(crossing(listen, first_row), powers, precision=lax.Precision.HIGHEST)

    interference = lax.map(row_pass, (listen_blocks, starts)).reshape(USERS, CHANNELS)
    signal = ARRAY_GAIN * own_gain[:, None] * powers
    denominator = NOISE_POWER + interference
    quality = signal / denominator
    user_scale = WEIGHT_UNIT * weight.astype(jnp.float32)
    marginal = user_scale[:, None] * jnp.exp(-fairness.astype(jnp.float32)[:, None] * jnp.log(quality)) / denominator
    pressure = marginal * quality
    pressure_blocks = pressure.reshape(blocks, block_rows, CHANNELS)

    def column_pass(running, inputs):
        listen, first_row, pressure_block = inputs
        gain_tile = crossing(listen, first_row)
        pushed = lax.dot_general(gain_tile, pressure_block, (((0,), (0,)), ((), ())), precision=lax.Precision.HIGHEST)
        return running + pushed, None

    reaction, _ = lax.scan(column_pass, jnp.zeros((USERS, CHANNELS), jnp.float32), (listen_blocks, starts, pressure_blocks))
    gradient = ARRAY_GAIN * own_gain[:, None] * marginal - reaction
    target = PEAK_POWER * jax.nn.sigmoid(gradient)
    step_size = step_code[0].astype(jnp.float32) / 4096.0
    new_power = powers + step_size * (target - powers)
    duality_gap = (jnp.sum(PEAK_POWER * jnp.maximum(gradient, 0.0) - gradient * powers) / (USERS * CHANNELS)).reshape(1)
    return quality, gradient, new_power, duality_gap
```

```python
import jax
import jax.numpy as jnp
from jax import lax
from jax.experimental import pallas as pl
from jax.experimental.pallas import tpu as pltpu
from jax.sharding import Mesh
from jax.sharding import PartitionSpec as P

NOISE_POWER = 0.05
ARRAY_GAIN = 32.0
WEIGHT_UNIT = 1.0 / 16.0
PEAK_POWER = 1.0

AXES = ("zlo", "x", "y", "zhi", "core")
Z = ("zhi", "zlo")
XY = ("x", "y")
NZ, NXY = 16, 16
BLOCK, BANDS = 64, 128
HALF = NZ * BLOCK
ROWS = NXY * BLOCK
USERS = 32768
VMEM_LIMIT = 48 * 1024 * 1024
F32, BF16 = jnp.float32, jnp.bfloat16


def whole():
    return pl.BlockSpec(memory_space=pltpu.VMEM)


def call(kernel, outs, n_in, flops=0, bytes_accessed=1 << 20, smem=(), scratch=()):
    specs = [pl.BlockSpec(memory_space=pltpu.SMEM) if i in smem else whole() for i in range(n_in)]
    many = isinstance(outs, (list, tuple))
    return pl.pallas_call(
        kernel,
        out_shape=outs,
        in_specs=specs,
        out_specs=[whole() for _ in outs] if many else whole(),
        scratch_shapes=scratch,
        compiler_params=pltpu.CompilerParams(vmem_limit_bytes=VMEM_LIMIT),
        cost_estimate=pl.CostEstimate(flops=flops, bytes_accessed=bytes_accessed, transcendentals=0),
    )


def shape(*dims, dtype=F32):
    return jax.ShapeDtypeStruct(dims, dtype)


def split_norm(norm):
    low = norm & 511
    odd = low & 1
    return norm - low, low - odd, odd


def pack_kernel(sender_ref, listener_ref, powers_ref, sent_ref, heard_ref):
    sx, sy = sender_ref[0:1, :], sender_ref[1:2, :]
    lx, ly = listener_ref[0:1, :], listener_ref[1:2, :]
    one = jnp.ones_like(sx)
    s1, s2, s3 = split_norm(sx * sx + sy * sy)
    l1, l2, l3 = split_norm(lx * lx + ly * ly + 1)
    sent = jnp.concatenate([-2 * sx, -2 * sy, one, one, one, s1, s2, s3], axis=0).astype(F32)
    heard = jnp.concatenate([lx, ly, l1, l2, l3, one, one, one], axis=0).astype(F32)
    pad = jnp.zeros_like(sent)
    sent_ref[0:BLOCK, :] = powers_ref[...]
    sent_ref[BLOCK : BLOCK + 8, :] = jnp.concatenate([sent, pad], axis=1)
    heard_ref[...] = jnp.concatenate([heard, pad], axis=1)


def spread(parts, row):
    pieces = []
    for k in range(0, 16, 2):
        left = parts[k, row : row + 8, 0:BLOCK]
        right = parts[k + 1, row : row + 8, 0:BLOCK]
        pieces.append(jnp.concatenate([left, right], axis=1))
    features = jnp.concatenate(pieces, axis=1)
    return jnp.concatenate([features, jnp.zeros_like(features)], axis=0).astype(BF16)


def split(value):
    high = value.astype(BF16)
    low = (value - high.astype(F32)).astype(BF16)
    return high, low


def interfere_kernel(first, place_ref, sent_ref, heard_ref, *rest):
    if first:
        total_ref, high_ref, low_ref = rest
    else:
        before_ref, total_ref, high_ref, low_ref = rest
    x, y, zlo, zhi, core, source_core = (place_ref[i] for i in range(6))
    senders = spread(sent_ref, BLOCK)
    listeners = spread(heard_ref, 0)
    powers = sent_ref[:, 0:BLOCK, :].reshape(HALF, BANDS)
    power_high, power_low = split(powers)
    power_both = jnp.concatenate([power_high, power_low], axis=1)
    tile_rows, tile_cols = 256, 128
    receiver_base = zlo * 4096 + zhi * 128 + core * 64
    sender_base = y * 8192 + source_core * 2048 + x * 64
    for r in range(0, ROWS, tile_rows):
        row = lax.broadcasted_iota(jnp.int32, (tile_rows, tile_cols), 0) + r
        block = row >> 6
        row_id = receiver_base + (block >> 2) * 1024 + (block & 3) * 256 + (row & 63)
        for c in range(0, HALF, tile_cols):
            col = lax.broadcasted_iota(jnp.int32, (1, tile_cols), 1) + c
            zed = col >> 6
            col_id = sender_base + (zed >> 3) * 4096 + (zed & 7) * 256 + (col & 63)
            square = lax.dot_general(
                listeners[:, r : r + tile_rows],
                senders[:, c : c + tile_cols],
                (((0,), (0,)), ((), ())),
                preferred_element_type=F32,
            )
            guess = pl.reciprocal(square, approx=True)
            gain = guess * (2.0 - square * guess)
            gain = jnp.where(row_id == col_id, 0.0, gain)
            high, low = split(gain)
            high_ref[r : r + tile_rows, c : c + tile_cols] = high
            low_ref[r : r + tile_rows, c : c + tile_cols] = low
        product = jnp.dot(high_ref[r : r + tile_rows, :], power_both, preferred_element_type=F32)
        product = product + jnp.dot(
            low_ref[r : r + tile_rows, :], power_both, preferred_element_type=F32
        )
        part = product[:, :BANDS] + product[:, BANDS:]
        if not first:
            part = part + before_ref[r : r + tile_rows, :]
        total_ref[r : r + tile_rows, :] = part


def react_kernel(pressure_ref, high_ref, low_ref, pushed_ref):
    pressure = pressure_ref[...].reshape(ROWS, BANDS).T
    pressure_high, pressure_low = split(pressure)
    both = jnp.concatenate([pressure_high, pressure_low], axis=0)
    step = 256
    for c in range(0, HALF, step):
        product = jnp.dot(both, high_ref[:, c : c + step], preferred_element_type=F32)
        product = product + jnp.dot(both, low_ref[:, c : c + step], preferred_element_type=F32)
        pushed_ref[c : c + step, :] = (product[:BANDS, :] + product[BANDS:, :]).T


def add_blocks(ref, count):
    total = ref[0]
    for k in range(1, count):
        total = total + ref[k]
    return total


def derive_kernel(parts_ref, mine_ref, listener_ref, user_ref, quality_ref, own_ref, pressure_ref):
    interference = add_blocks(parts_ref, NXY)
    powers = mine_ref[0:BLOCK, :]
    sx = -0.5 * mine_ref[BLOCK : BLOCK + 1, 0:BLOCK]
    sy = -0.5 * mine_ref[BLOCK + 1 : BLOCK + 2, 0:BLOCK]
    dx = listener_ref[0:1, :].astype(F32) - sx
    dy = listener_ref[1:2, :].astype(F32) - sy
    own_gain = 1.0 / (1.0 + dx * dx + dy * dy)
    weight = WEIGHT_UNIT * user_ref[0:1, :].astype(F32)
    fair = user_ref[1:2, :].astype(F32)
    rows = jnp.concatenate([own_gain, weight, fair, jnp.zeros((5, BLOCK), F32)], axis=0)
    rows = jnp.concatenate([rows, jnp.zeros_like(rows)], axis=1)
    columns = jnp.concatenate([rows, jnp.zeros((120, 128), F32)], axis=0).T
    own_gain = columns[0:BLOCK, 0:1]
    weight = columns[0:BLOCK, 1:2]
    fair = columns[0:BLOCK, 2:3]
    signal = ARRAY_GAIN * own_gain * powers
    denominator = NOISE_POWER + interference
    quality = signal / denominator
    marginal = weight * jnp.exp(-fair * jnp.log(quality)) / denominator
    quality_ref[...] = quality
    own_ref[...] = ARRAY_GAIN * own_gain * marginal
    pressure_ref[...] = marginal * quality


def finish_kernel(step_ref, parts_ref, own_ref, powers_ref, gradient_ref, power_ref, gap_ref):
    gradient = own_ref[...] - add_blocks(parts_ref, NZ)
    powers = powers_ref[...]
    target = PEAK_POWER * jax.nn.sigmoid(gradient)
    step_size = step_ref[0].astype(F32) / 4096.0
    gradient_ref[...] = gradient
    power_ref[...] = powers + step_size * (target - powers)
    gap = PEAK_POWER * jnp.maximum(gradient, 0.0) - gradient * powers
    gap_ref[...] = jnp.sum(gap, axis=0, keepdims=True)


def share(value, axes, count):
    return lax.all_to_all(jnp.broadcast_to(value[None], (count, *value.shape)), axes, 0, 0)


def per_device(sender_xy, listener_xy, powers, weight, fairness, step_code):
    at = {name: lax.axis_index(name).astype(jnp.int32) for name in AXES}
    place = [at["x"], at["y"], at["zlo"], at["zhi"], at["core"]]
    to_receiver = [((b % 32) * 16 + b // 32, b) for b in range(512)]
    to_sender = [(d, s) for s, d in to_receiver]
    swap = [(0, 1), (1, 0)]

    sent, heard = call(pack_kernel, (shape(BLOCK + 8, BANDS), shape(8, 128)), 3)(
        sender_xy, listener_xy, powers
    )
    mine = lax.ppermute(sent, AXES, to_receiver)
    listeners = share(heard, XY, NXY)
    near = share(sent, Z, NZ)
    far = lax.ppermute(near, "core", swap)

    gains = shape(ROWS, HALF, dtype=BF16)
    work = dict(flops=2 * ROWS * HALF * 512, bytes_accessed=1 << 23)
    outs = (shape(ROWS, BANDS), gains, gains)
    near_place = jnp.stack([*place, at["core"]])
    far_place = jnp.stack([*place, 1 - at["core"]])
    part, near_high, near_low = call(
        lambda *refs: interfere_kernel(True, *refs), outs, 3, smem=(0,), **work
    )(near_place, near, listeners)
    part, far_high, far_low = call(
        lambda *refs: interfere_kernel(False, *refs), outs, 4, smem=(0,), **work
    )(far_place, far, listeners, part)

    parts = lax.all_to_all(part.reshape(NXY, BLOCK, BANDS), XY, 0, 0)
    users = jnp.stack([weight, fairness])
    block = shape(BLOCK, BANDS)
    quality, own, pressure = call(derive_kernel, (block, block, block), 4)(
        parts, mine, listener_xy, users
    )
    own_here = lax.ppermute(own, AXES, to_sender)
    pressures = share(pressure, XY, NXY)

    react = call(react_kernel, shape(HALF, BANDS), 3, **work)
    pushed_far = react(pressures, far_high, far_low)
    pushed_far = lax.ppermute(pushed_far, "core", swap)
    pushed_near = react(pressures, near_high, near_low)
    pushed = pushed_near + pushed_far
    parts = lax.all_to_all(pushed.reshape(NZ, BLOCK, BANDS), Z, 0, 0)
    gradient, new_power, gap = call(finish_kernel, (block, block, shape(1, BANDS)), 4, smem=(0,))(
        step_code, parts, own_here, powers
    )
    gap = jnp.sum(share(gap, (*Z, "core"), 2 * NZ), axis=0)
    gap = jnp.sum(share(gap, XY, NXY))
    return quality, gradient, new_power, (gap / (USERS * BANDS)).reshape(1)


def solution(mesh):
    sizes = (8, 4, 4, 2, 2)
    fine = Mesh(mesh.devices.reshape(sizes), AXES)
    rx, tx = ("zlo", "x"), ("y", "zhi", "core")
    by_sender, by_receiver = (*tx, *rx), (*rx, *tx)
    return jax.shard_map(
        per_device,
        mesh=fine,
        in_specs=(
            P(None, by_sender),
            P(None, by_receiver),
            P(by_sender, None),
            P(by_receiver),
            P(by_receiver),
            P(),
        ),
        out_specs=(P(by_receiver, None), P(by_sender, None), P(by_sender, None), P()),
        check_vma=False,
    )
```

```python
import functools

import jax
import jax.numpy as jnp
from jax import lax
from jax.experimental import pallas as pl
from jax.experimental.pallas import tpu as pltpu
from jax.sharding import Mesh
from jax.sharding import PartitionSpec as P

NOISE_POWER = 0.05
ARRAY_GAIN = 32.0
WEIGHT_UNIT = 1.0 / 16.0
PEAK_POWER = 1.0

AXES = ("z2", "z1", "z0", "x", "y", "zhi", "core")
SIZES = (2, 2, 2, 4, 4, 2, 2)
EVEN = ("zhi", "z2", "z1")
Z = ("z0", *EVEN)
XY = ("x", "y")
NZ, NXY = 16, 16
BLOCK, BANDS = 64, 128
SENT = BLOCK + 8
HALF = NZ * BLOCK
ROWS = NXY * BLOCK
USERS = 32768
VMEM_LIMIT = 20 * 1024 * 1024
F32, BF16 = jnp.float32, jnp.bfloat16
PLACE = ("x", "y", "z0", "z2", "z1", "zhi", "core")


def whole():
    return pl.BlockSpec(memory_space=pltpu.VMEM)


def call(kernel, outs, n_in, flops=0, bytes_accessed=1 << 20, smem=()):
    def spec(i):
        return pl.BlockSpec(memory_space=pltpu.SMEM) if i in smem else whole()

    many = isinstance(outs, (list, tuple))
    return pl.pallas_call(
        kernel,
        out_shape=outs,
        in_specs=[spec(i) for i in range(n_in)],
        out_specs=[whole() for _ in outs] if many else whole(),
        compiler_params=pltpu.CompilerParams(vmem_limit_bytes=VMEM_LIMIT),
        cost_estimate=pl.CostEstimate(flops=flops, bytes_accessed=bytes_accessed, transcendentals=0),
    )


def shape(*dims, dtype=F32):
    return jax.ShapeDtypeStruct(dims, dtype)


def split_norm(norm):
    low = norm & 511
    odd = low & 1
    return norm - low, low - odd, odd


def pack_kernel(sender_ref, listener_ref, powers_ref, sent_ref, heard_ref):
    sx, sy = sender_ref[0:1, :], sender_ref[1:2, :]
    lx, ly = listener_ref[0:1, :], listener_ref[1:2, :]
    one = jnp.ones_like(sx)
    s1, s2, s3 = split_norm(sx * sx + sy * sy)
    l1, l2, l3 = split_norm(lx * lx + ly * ly + 1)
    sent = jnp.concatenate([-2 * sx, -2 * sy, one, one, one, s1, s2, s3], axis=0).astype(F32)
    heard = jnp.concatenate([lx, ly, l1, l2, l3, one, one, one], axis=0).astype(F32)
    pad = jnp.zeros_like(sent)
    sent = jnp.concatenate([sent, pad], axis=1)
    heard_ref[...] = jnp.concatenate([heard, pad], axis=1)
    powers = powers_ref[...]
    for k in range(NZ):
        sent_ref[k, 0:BLOCK, :] = powers
        sent_ref[k, BLOCK:SENT, :] = sent


def spread(parts, row, index):
    pieces = []
    for k in range(0, 16, 2):
        left = parts[index(k), row : row + 8, 0:BLOCK]
        right = parts[index(k + 1), row : row + 8, 0:BLOCK]
        pieces.append(jnp.concatenate([left, right], axis=1))
    features = jnp.concatenate(pieces, axis=1)
    return jnp.concatenate([features, jnp.zeros_like(features)], axis=0).astype(BF16)


def split(value):
    high = value.astype(BF16)
    low = (value - high.astype(F32)).astype(BF16)
    return high, low


def interfere_kernel(first, place_ref, sent_ref, heard_ref, *rest):
    if first:
        total_ref, high_ref, low_ref = rest
    else:
        near_ref, before_ref, total_ref, high_ref, low_ref = rest
    x, y, z0, z2, z1, zhi, core = (place_ref[i] for i in range(7))
    source_core = core if first else 1 - core
    senders = spread(sent_ref, BLOCK, lambda k: k)
    listeners = spread(heard_ref, 0, lambda k: (((k & 3) ^ y) << 2) | ((k >> 2) ^ x))
    powers = sent_ref[:, 0:BLOCK, :].reshape(HALF, BANDS)
    power_high, power_low = split(powers)
    power_both = jnp.concatenate([power_high, power_low], axis=1)
    tile_rows, tile_cols = 256, 128
    per_tile = tile_rows // BLOCK
    receiver_base = (z2 * 4 + z1 * 2 + z0) * 4096 + zhi * 128 + core * 64
    sender_base = y * 8192 + source_core * 2048 + x * 64
    for r in range(0, ROWS, tile_rows):
        row = lax.broadcasted_iota(jnp.int32, (tile_rows, tile_cols), 0) + r
        block = row >> 6
        row_id = receiver_base + (block >> 2) * 1024 + (block & 3) * 256 + (row & 63)
        for c in range(0, HALF, tile_cols):
            col = lax.broadcasted_iota(jnp.int32, (1, tile_cols), 1) + c
            zed = col >> 6
            zlo = ((zed >> 1) & 1) * 4 + (zed & 1) * 2 + (zed >> 3)
            col_id = sender_base + ((zed >> 2) & 1) * 4096 + zlo * 256 + (col & 63)
            square = lax.dot_general(
                listeners[:, r : r + tile_rows],
                senders[:, c : c + tile_cols],
                (((0,), (0,)), ((), ())),
                preferred_element_type=F32,
            )
            guess = pl.reciprocal(square, approx=True)
            gain = guess * (2.0 - square * guess)
            gain = jnp.where(row_id == col_id, 0.0, gain)
            high, low = split(gain)
            high_ref[r : r + tile_rows, c : c + tile_cols] = high
            low_ref[r : r + tile_rows, c : c + tile_cols] = low
        product = jnp.dot(high_ref[r : r + tile_rows, :], power_both, preferred_element_type=F32)
        product = product + jnp.dot(
            low_ref[r : r + tile_rows, :], power_both, preferred_element_type=F32
        )
        part = product[:, :BANDS] + product[:, BANDS:]
        if first:
            total_ref[r : r + tile_rows, :] = part
        else:
            k = r // BLOCK
            part = part + before_ref[r : r + tile_rows, :]
            total_ref[k : k + per_tile, 0:BLOCK, :] = part.reshape(per_tile, BLOCK, BANDS)
    if not first:
        for k in range(NXY):
            there_x, there_y = k >> 2, k & 3
            at = (there_y & 1) * 8 + z0 * 4 + (there_x & 1) * 2 + (there_y >> 1)
            total_ref[k, BLOCK:, :] = jnp.where(
                core == there_x >> 1, near_ref[at], sent_ref[at]
            )


def react_kernel(place_ref, pressure_ref, high_ref, low_ref, pushed_ref, *, other):
    pressure = pressure_ref[...].reshape(ROWS, BANDS).T
    pressure_high, pressure_low = split(pressure)
    both = jnp.concatenate([pressure_high, pressure_low], axis=0)
    parity = 1 - place_ref[2] if other else place_ref[2]
    step = 256
    for c in range(0, HALF // 2, step):
        columns = pl.ds(pl.multiple_of(parity * (HALF // 2) + c, step), step)
        product = jnp.dot(both, high_ref[:, columns], preferred_element_type=F32)
        product = product + jnp.dot(both, low_ref[:, columns], preferred_element_type=F32)
        pushed_ref[c : c + step, :] = (product[:BANDS, :] + product[BANDS:, :]).T


def add_kernel(*refs):
    total = refs[0][...]
    for ref in refs[1:-1]:
        total = total + ref[...]
    refs[-1][...] = total


def add(*parts):
    size = 4 * parts[0].size
    return call(add_kernel, shape(*parts[0].shape), len(parts), parts[0].size, 3 * size)(*parts)


def add_blocks(ref, count):
    total = ref[0, 0:BLOCK, :]
    for k in range(1, count):
        total = total + ref[k, 0:BLOCK, :]
    return total


def derive_kernel(
    place_ref, parts_ref, listener_ref, weight_ref, fair_ref, quality_ref, own_ref, pressure_ref
):
    interference = add_blocks(parts_ref, NXY)
    z2, z1, zhi, core = (place_ref[i] for i in range(3, 7))
    source = (zhi * 2 + core) * 4 + z2 * 2 + z1
    powers = parts_ref[source, BLOCK : 2 * BLOCK, :]
    place = -0.5 * parts_ref[source, 2 * BLOCK :, :]
    sx, sy = place[0:1, 0:BLOCK], place[1:2, 0:BLOCK]
    dx = listener_ref[0:1, :].astype(F32) - sx
    dy = listener_ref[1:2, :].astype(F32) - sy
    own_gain = 1.0 / (1.0 + dx * dx + dy * dy)
    weight = WEIGHT_UNIT * weight_ref[...].astype(F32)
    fair = fair_ref[...].astype(F32)
    rows = jnp.concatenate([own_gain, weight, fair, jnp.zeros((5, BLOCK), F32)], axis=0)
    rows = jnp.concatenate([rows, jnp.zeros_like(rows)], axis=1)
    columns = jnp.concatenate([rows, jnp.zeros((120, 128), F32)], axis=0).T
    own_gain = columns[0:BLOCK, 0:1]
    weight = columns[0:BLOCK, 1:2]
    fair = columns[0:BLOCK, 2:3]
    signal = ARRAY_GAIN * own_gain * powers
    denominator = NOISE_POWER + interference
    quality = signal / denominator
    marginal = weight * jnp.exp(-fair * jnp.log(quality)) / denominator
    quality_ref[...] = quality
    own_ref[...] = ARRAY_GAIN * own_gain * marginal
    pressure = marginal * quality
    for k in range(NXY):
        pressure_ref[k] = pressure


def finish_kernel(step_ref, parts_ref, own_ref, powers_ref, gradient_ref, power_ref, gap_ref):
    gradient = own_ref[...] - add_blocks(parts_ref, NZ // 2)
    powers = powers_ref[...]
    target = PEAK_POWER * jax.nn.sigmoid(gradient)
    step_size = step_ref[0].astype(F32) / 4096.0
    gradient_ref[...] = gradient
    power_ref[...] = powers + step_size * (target - powers)
    gap = PEAK_POWER * jnp.maximum(gradient, 0.0) - gradient * powers
    gap = jnp.sum(gap, axis=0, keepdims=True)
    for k in range(2 * NZ):
        gap_ref[k] = gap


def share(value, axes, count):
    return lax.all_to_all(jnp.broadcast_to(value[None], (count, *value.shape)), axes, 0, 0)


def per_device(sender_xy, listener_xy, powers, weight, fairness, step_code):
    place = jnp.stack([lax.axis_index(name).astype(jnp.int32) for name in PLACE])
    to_sender = [(b, (b % 32) * 16 + b // 32) for b in range(512)]
    swap = [(0, 1), (1, 0)]

    sent, heard = call(pack_kernel, (shape(NZ, SENT, BANDS), shape(8, 128)), 3)(
        sender_xy, listener_xy, powers
    )
    near = lax.all_to_all(sent, Z, 0, 0)
    for axis in XY:
        for bit in (1, 2):
            other = lax.ppermute(heard, axis, [(i, i ^ bit) for i in range(4)])
            heard = jnp.concatenate([heard, other], axis=0)
    near, heard = lax.optimization_barrier((near, heard))
    listeners = heard.reshape(NXY, 8, 128)
    far = lax.ppermute(near, "core", swap)

    gains = shape(ROWS, HALF, dtype=BF16)
    work = dict(flops=2 * ROWS * HALF * 512, bytes_accessed=1 << 23)
    part, near_high, near_low = call(
        lambda *refs: interfere_kernel(True, *refs), (shape(ROWS, BANDS), gains, gains), 3, smem=(0,), **work
    )(place, near, listeners)
    parts, far_high, far_low = call(
        lambda *refs: interfere_kernel(False, *refs),
        (shape(NXY, BLOCK + SENT, BANDS), gains, gains),
        5,
        smem=(0,),
        **work,
    )(place, far, listeners, near, part)

    parts = lax.all_to_all(parts, XY, 0, 0)
    block = shape(BLOCK, BANDS)
    quality, own, pressure = call(
        derive_kernel, (block, block, shape(NXY, BLOCK, BANDS)), 5, smem=(0,)
    )(place, parts, listener_xy, weight[None], fairness[None])
    pressures = lax.all_to_all(pressure, XY, 0, 0)

    def react(pressures, high, low, other):
        kernel = functools.partial(react_kernel, other=other)
        quarter = dict(flops=work["flops"] // 2, bytes_accessed=1 << 21)
        return call(kernel, shape(HALF // 2, BANDS), 4, smem=(0,), **quarter)(
            place, pressures, high, low
        )

    across = lax.ppermute(react(pressures, far_high, far_low, True), "core", swap)
    pushed = add(react(pressures, near_high, near_low, True), across)
    pressures, pushed = lax.optimization_barrier((pressures, pushed))
    from_neighbour = lax.ppermute(pushed, "z0", swap)
    across = lax.ppermute(react(pressures, far_high, far_low, False), "core", swap)
    pushed = add(react(pressures, near_high, near_low, False), across, from_neighbour)
    own_here = lax.ppermute(own, AXES, to_sender)
    parts = lax.all_to_all(pushed.reshape(NZ // 2, BLOCK, BANDS), EVEN, 0, 0)
    gradient, new_power, gap = call(
        finish_kernel, (block, block, shape(2 * NZ, 1, BANDS)), 4, smem=(0,)
    )(step_code, parts, own_here, powers)
    gap = jnp.sum(lax.all_to_all(gap, (*Z, "core"), 0, 0), axis=0)
    gap = lax.all_to_all(jnp.broadcast_to(gap[None], (NXY, 1, BANDS)), XY, 0, 0)
    return quality, gradient, new_power, (jnp.sum(gap) / (USERS * BANDS)).reshape(1)


def solution(mesh):
    fine = Mesh(mesh.devices.reshape(SIZES), AXES)
    rx, tx = ("z2", "z1", "z0", "x"), ("y", "zhi", "core")
    by_sender, by_receiver = (*tx, *rx), (*rx, *tx)
    return jax.shard_map(
        per_device,
        mesh=fine,
        in_specs=(
            P(None, by_sender),
            P(None, by_receiver),
            P(by_sender, None),
            P(by_receiver),
            P(by_receiver),
            P(),
        ),
        out_specs=(P(by_receiver, None), P(by_sender, None), P(by_sender, None), P()),
        check_vma=False,
    )
```

```python
import functools

import jax
import jax.numpy as jnp
from jax import lax
from jax.experimental import pallas as pl
from jax.experimental.pallas import tpu as pltpu
from jax.sharding import Mesh
from jax.sharding import PartitionSpec as P

NOISE_POWER = 0.05
ARRAY_GAIN = 32.0
WEIGHT_UNIT = 1.0 / 16.0
PEAK_POWER = 1.0

AXES = ("z2", "z1", "z0", "x", "y", "zhi", "core")
SIZES = (2, 2, 2, 4, 4, 2, 2)
EVEN = ("zhi", "z2", "z1")
Z = ("z0", *EVEN)
XY = ("x", "y")
NZ, NXY = 16, 16
BLOCK, BANDS = 64, 128
SENT = BLOCK + 8
HALF = NZ * BLOCK
ROWS = NXY * BLOCK
USERS = 32768
VMEM_LIMIT = 20 * 1024 * 1024
F32, BF16 = jnp.float32, jnp.bfloat16
PLACE = ("x", "y", "z0", "z2", "z1", "zhi", "core")


def whole():
    return pl.BlockSpec(memory_space=pltpu.VMEM)


def call(kernel, outs, n_in, flops=0, bytes_accessed=1 << 20, smem=()):
    def spec(i):
        return pl.BlockSpec(memory_space=pltpu.SMEM) if i in smem else whole()

    many = isinstance(outs, (list, tuple))
    return pl.pallas_call(
        kernel,
        out_shape=outs,
        in_specs=[spec(i) for i in range(n_in)],
        out_specs=[whole() for _ in outs] if many else whole(),
        compiler_params=pltpu.CompilerParams(vmem_limit_bytes=VMEM_LIMIT),
        cost_estimate=pl.CostEstimate(flops=flops, bytes_accessed=bytes_accessed, transcendentals=0),
    )


def shape(*dims, dtype=F32):
    return jax.ShapeDtypeStruct(dims, dtype)


def split_norm(norm):
    low = norm & 511
    odd = low & 1
    return norm - low, low - odd, odd


def pack_kernel(info_ref, powers_ref, sent_ref, heard_ref):
    sx, sy, lx, ly = (info_ref[i : i + 1, :] for i in range(4))
    one = jnp.ones_like(sx)
    s1, s2, s3 = split_norm(sx * sx + sy * sy)
    l1, l2, l3 = split_norm(lx * lx + ly * ly + 1)
    sent = jnp.concatenate([-2 * sx, -2 * sy, one, one, one, s1, s2, s3], axis=0).astype(F32)
    heard = jnp.concatenate([lx, ly, l1, l2, l3, one, one, one], axis=0).astype(F32)
    pad = jnp.zeros_like(sent)
    sent = jnp.concatenate([sent, pad], axis=1)
    user = jnp.concatenate([info_ref[4:6, :].astype(F32), jnp.zeros((6, BLOCK), F32)], axis=0)
    heard_ref[...] = jnp.concatenate([heard, user], axis=1)
    powers = powers_ref[...]
    for k in range(NZ):
        sent_ref[k, 0:BLOCK, :] = powers
        sent_ref[k, BLOCK:SENT, :] = sent


def spread(parts, row, index):
    pieces = []
    for k in range(0, 16, 2):
        left = parts[index(k), row : row + 8, 0:BLOCK]
        right = parts[index(k + 1), row : row + 8, 0:BLOCK]
        pieces.append(jnp.concatenate([left, right], axis=1))
    features = jnp.concatenate(pieces, axis=1)
    return jnp.concatenate([features, jnp.zeros_like(features)], axis=0).astype(BF16)


def split(value):
    high = value.astype(BF16)
    low = (value - high.astype(F32)).astype(BF16)
    return high, low


def interfere_kernel(first, place_ref, sent_ref, heard_ref, *rest):
    if first:
        total_ref, high_ref, low_ref = rest
    else:
        before_ref, total_ref, high_ref, low_ref = rest
    x, y, z0, z2, z1, zhi, core = (place_ref[i] for i in range(7))
    source_core = core if first else 1 - core
    senders = spread(sent_ref, BLOCK, lambda k: k)
    listeners = spread(heard_ref, 0, lambda k: (((k & 3) ^ y) << 2) | ((k >> 2) ^ x))
    powers = sent_ref[:, 0:BLOCK, :].reshape(HALF, BANDS)
    power_high, power_low = split(powers)
    power_both = jnp.concatenate([power_high, power_low], axis=1)
    tile_rows, tile_cols = 256, 128
    receiver_base = zhi * 4096 + core * 2048 + (z2 * 4 + z1 * 2 + z0) * 256
    sender_base = y * 8192 + source_core * 2048 + x * 64
    for r in range(0, ROWS, tile_rows):
        row = lax.broadcasted_iota(jnp.int32, (tile_rows, tile_cols), 0) + r
        block = row >> 6
        row_id = receiver_base + (block & 3) * 8192 + (block >> 2) * 64 + (row & 63)
        for c in range(0, HALF, tile_cols):
            col = lax.broadcasted_iota(jnp.int32, (1, tile_cols), 1) + c
            zed = col >> 6
            zlo = ((zed >> 1) & 1) * 4 + (zed & 1) * 2 + (zed >> 3)
            col_id = sender_base + ((zed >> 2) & 1) * 4096 + zlo * 256 + (col & 63)
            square = lax.dot_general(
                listeners[:, r : r + tile_rows],
                senders[:, c : c + tile_cols],
                (((0,), (0,)), ((), ())),
                preferred_element_type=F32,
            )
            guess = pl.reciprocal(square, approx=True)
            gain = guess * (2.0 - square * guess)
            gain = jnp.where(row_id == col_id, 0.0, gain)
            high, low = split(gain)
            high_ref[r : r + tile_rows, c : c + tile_cols] = high
            low_ref[r : r + tile_rows, c : c + tile_cols] = low
        product = jnp.dot(high_ref[r : r + tile_rows, :], power_both, preferred_element_type=F32)
        product = product + jnp.dot(
            low_ref[r : r + tile_rows, :], power_both, preferred_element_type=F32
        )
        part = product[:, :BANDS] + product[:, BANDS:]
        if not first:
            part = part + before_ref[r : r + tile_rows, :]
        total_ref[r : r + tile_rows, :] = part


def turn_kernel(pressure_ref, both_ref):
    pressure = pressure_ref[...].reshape(ROWS, BANDS).T
    pressure_high, pressure_low = split(pressure)
    both_ref[0:BANDS, :] = pressure_high
    both_ref[BANDS:, :] = pressure_low


def react_kernel(place_ref, both_ref, high_ref, low_ref, pushed_ref, *, other):
    both = both_ref[...]
    parity = 1 - place_ref[2] if other else place_ref[2]
    step = 256
    for c in range(0, HALF // 2, step):
        columns = pl.ds(pl.multiple_of(parity * (HALF // 2) + c, step), step)
        product = jnp.dot(both, high_ref[:, columns], preferred_element_type=F32)
        product = product + jnp.dot(both, low_ref[:, columns], preferred_element_type=F32)
        pushed_ref[c : c + step, :] = (product[:BANDS, :] + product[BANDS:, :]).T


def join_kernel(a_ref, b_ref, out_ref):
    rows = a_ref.shape[0]
    out_ref[0:rows, :] = a_ref[...]
    out_ref[rows:, :] = b_ref[...]


def join(a, b):
    rows, lanes = a.shape
    return call(join_kernel, shape(2 * rows, lanes), 2, 0, 16 * a.size)(a, b)


def add_kernel(*refs):
    total = refs[0][...]
    for ref in refs[1:-1]:
        total = total + ref[...]
    refs[-1][...] = total


def add(*parts):
    size = 4 * parts[0].size
    return call(add_kernel, shape(*parts[0].shape), len(parts), parts[0].size, 3 * size)(*parts)


def add_blocks(ref, count):
    total = ref[0, 0:BLOCK, :]
    for k in range(1, count):
        total = total + ref[k, 0:BLOCK, :]
    return total


def derive_kernel(
    parts_ref, powers_ref, sender_ref, heard_ref, quality_ref, own_ref, pressure_ref
):
    interference = add_blocks(parts_ref, NXY)
    powers = powers_ref[...]
    dx = heard_ref[0:1, 0:BLOCK] - sender_ref[0:1, :].astype(F32)
    dy = heard_ref[1:2, 0:BLOCK] - sender_ref[1:2, :].astype(F32)
    own_gain = 1.0 / (1.0 + dx * dx + dy * dy)
    weight = WEIGHT_UNIT * heard_ref[0:1, BLOCK:]
    fair = heard_ref[1:2, BLOCK:]
    rows = jnp.concatenate([own_gain, weight, fair, jnp.zeros((5, BLOCK), F32)], axis=0)
    rows = jnp.concatenate([rows, jnp.zeros_like(rows)], axis=1)
    columns = jnp.concatenate([rows, jnp.zeros((120, 128), F32)], axis=0).T
    own_gain = columns[0:BLOCK, 0:1]
    weight = columns[0:BLOCK, 1:2]
    fair = columns[0:BLOCK, 2:3]
    signal = ARRAY_GAIN * own_gain * powers
    denominator = NOISE_POWER + interference
    quality = signal / denominator
    marginal = weight * jnp.exp(-fair * jnp.log(quality)) / denominator
    quality_ref[...] = quality
    own_ref[...] = ARRAY_GAIN * own_gain * marginal
    pressure = marginal * quality
    for k in range(NXY):
        pressure_ref[k] = pressure


def finish_kernel(step_ref, parts_ref, own_ref, powers_ref, gradient_ref, power_ref, gap_ref):
    gradient = own_ref[...] - add_blocks(parts_ref, NZ // 2)
    powers = powers_ref[...]
    target = PEAK_POWER * jax.nn.sigmoid(gradient)
    step_size = step_ref[0].astype(F32) / 4096.0
    gradient_ref[...] = gradient
    power_ref[...] = powers + step_size * (target - powers)
    gap = PEAK_POWER * jnp.maximum(gradient, 0.0) - gradient * powers
    gap = jnp.sum(gap, axis=0, keepdims=True)
    for k in range(2 * NZ):
        gap_ref[k] = gap


def share(value, axes, count):
    return lax.all_to_all(jnp.broadcast_to(value[None], (count, *value.shape)), axes, 0, 0)


def per_device(sender_xy, listener_xy, powers, weight, fairness, step_code):
    place = jnp.stack([lax.axis_index(name).astype(jnp.int32) for name in PLACE])
    to_sender = [(b, (b % 32) * 16 + b // 32) for b in range(512)]
    to_receiver = [(s, b) for b, s in to_sender]
    swap = [(0, 1), (1, 0)]

    rows = [sender_xy, listener_xy, weight[None], fairness[None], jnp.zeros((2, BLOCK), jnp.int32)]
    info = jnp.concatenate(rows, axis=0)
    sent, heard = call(pack_kernel, (shape(NZ, SENT, BANDS), shape(8, 128)), 2)(info, powers)
    mine = heard = lax.ppermute(heard, AXES, to_sender)
    near = lax.all_to_all(sent, Z, 0, 0)
    for axis in XY:
        for bit in (1, 2):
            other = lax.ppermute(heard, axis, [(i, i ^ bit) for i in range(4)])
            heard = join(heard, other)
    near, heard = lax.optimization_barrier((near, heard))
    listeners = heard.reshape(NXY, 8, 128)
    far = lax.ppermute(near, "core", swap)

    gains = shape(ROWS, HALF, dtype=BF16)
    work = dict(flops=2 * ROWS * HALF * 512, bytes_accessed=1 << 23)
    part, near_high, near_low = call(
        lambda *refs: interfere_kernel(True, *refs), (shape(ROWS, BANDS), gains, gains), 3, smem=(0,), **work
    )(place, near, listeners)
    parts, far_high, far_low = call(
        lambda *refs: interfere_kernel(False, *refs),
        (shape(ROWS, BANDS), gains, gains),
        4,
        smem=(0,),
        **work,
    )(place, far, listeners, part)

    parts = lax.all_to_all(parts.reshape(NXY, BLOCK, BANDS), XY, 0, 0)
    block = shape(BLOCK, BANDS)
    quality, own, pressure = call(
        derive_kernel, (block, block, shape(NXY, BLOCK, BANDS)), 4
    )(parts, powers, sender_xy, mine)
    pressures = lax.all_to_all(pressure, XY, 0, 0)
    pressures = call(turn_kernel, shape(2 * BANDS, ROWS, dtype=BF16), 1)(pressures)

    def react(pressures, high, low, other):
        kernel = functools.partial(react_kernel, other=other)
        quarter = dict(flops=work["flops"] // 2, bytes_accessed=1 << 21)
        return call(kernel, shape(HALF // 2, BANDS), 4, smem=(0,), **quarter)(
            place, pressures, high, low
        )

    across = lax.ppermute(react(pressures, far_high, far_low, True), "core", swap)
    pushed = add(react(pressures, near_high, near_low, True), across)
    pressures, pushed = lax.optimization_barrier((pressures, pushed))
    from_neighbour = lax.ppermute(pushed, "z0", swap)
    across = lax.ppermute(react(pressures, far_high, far_low, False), "core", swap)
    pushed = add(react(pressures, near_high, near_low, False), across, from_neighbour)
    quality = lax.ppermute(quality, AXES, to_receiver)
    parts = lax.all_to_all(pushed.reshape(NZ // 2, BLOCK, BANDS), EVEN, 0, 0)
    gradient, new_power, gap = call(
        finish_kernel, (block, block, shape(2 * NZ, 1, BANDS)), 4, smem=(0,)
    )(step_code, parts, own, powers)
    gap = jnp.sum(lax.all_to_all(gap, (*Z, "core"), 0, 0), axis=0)
    gap = lax.all_to_all(jnp.broadcast_to(gap[None], (NXY, 1, BANDS)), XY, 0, 0)
    return quality, gradient, new_power, (jnp.sum(gap) / (USERS * BANDS)).reshape(1)


def solution(mesh):
    fine = Mesh(mesh.devices.reshape(SIZES), AXES)
    rx, tx = ("z2", "z1", "z0", "x"), ("y", "zhi", "core")
    by_sender, by_receiver = (*tx, *rx), (*rx, *tx)
    return jax.shard_map(
        per_device,
        mesh=fine,
        in_specs=(
            P(None, by_sender),
            P(None, by_receiver),
            P(by_sender, None),
            P(by_receiver),
            P(by_receiver),
            P(),
        ),
        out_specs=(P(by_receiver, None), P(by_sender, None), P(by_sender, None), P()),
        check_vma=False,
    )
```

```python
import jax
import jax.numpy as jnp
from jax import lax
from jax.experimental import pallas as pl
from jax.experimental.pallas import tpu as pltpu
from jax.sharding import Mesh
from jax.sharding import PartitionSpec as P

NOISE_POWER = 0.05
ARRAY_GAIN = 32.0
WEIGHT_UNIT = 1.0 / 16.0
PEAK_POWER = 1.0

AXES = ("z2", "z1", "z0", "x", "y", "zhi", "core")
SIZES = (2, 2, 2, 4, 4, 2, 2)
EVEN = ("zhi", "z2", "z1")
Z = ("z0", *EVEN)
XY = ("x", "y")
NZ, NXY = 16, 16
BLOCK, BANDS = 64, 128
SENT = BLOCK + 8
HALF = NZ * BLOCK
WIDE = HALF // 2
ROWS = NXY * BLOCK
USERS = 32768
VMEM_LIMIT = 20 * 1024 * 1024
F32, BF16 = jnp.float32, jnp.bfloat16
PLACE = ("x", "y", "z0", "z2", "z1", "zhi", "core")


def whole():
    return pl.BlockSpec(memory_space=pltpu.VMEM)


def call(kernel, outs, n_in, flops=0, bytes_accessed=1 << 20, smem=()):
    def spec(i):
        return pl.BlockSpec(memory_space=pltpu.SMEM) if i in smem else whole()

    many = isinstance(outs, (list, tuple))
    return pl.pallas_call(
        kernel,
        out_shape=outs,
        in_specs=[spec(i) for i in range(n_in)],
        out_specs=[whole() for _ in outs] if many else whole(),
        compiler_params=pltpu.CompilerParams(vmem_limit_bytes=VMEM_LIMIT),
        cost_estimate=pl.CostEstimate(flops=flops, bytes_accessed=bytes_accessed, transcendentals=0),
    )


def shape(*dims, dtype=F32):
    return jax.ShapeDtypeStruct(dims, dtype)


def split_norm(norm):
    low = norm & 511
    odd = low & 1
    return norm - low, low - odd, odd


def pack_kernel(info_ref, powers_ref, sent_ref, heard_ref, mine_ref):
    sx, sy, lx, ly = (info_ref[i : i + 1, :] for i in range(4))
    one = jnp.ones_like(sx)
    s1, s2, s3 = split_norm(sx * sx + sy * sy)
    l1, l2, l3 = split_norm(lx * lx + ly * ly + 1)
    sent = jnp.concatenate([-2 * sx, -2 * sy, one, one, one, s1, s2, s3], axis=0).astype(F32)
    heard = jnp.concatenate([lx, ly, l1, l2, l3, one, one, one], axis=0).astype(F32)
    pad = jnp.zeros_like(sent)
    sent = jnp.concatenate([sent, pad], axis=1)
    heard_ref[...] = jnp.concatenate([heard, pad], axis=1)
    powers = powers_ref[...]
    mine_ref[0:BLOCK, :] = powers
    mine_ref[BLOCK:, :] = sent
    for k in range(NZ):
        sent_ref[k, 0:BLOCK, :] = powers
        sent_ref[k, BLOCK:SENT, :] = sent


def spread(parts, row, index):
    pieces = []
    for k in range(0, 16, 2):
        left = parts[index(k), row : row + 8, 0:BLOCK]
        right = parts[index(k + 1), row : row + 8, 0:BLOCK]
        pieces.append(jnp.concatenate([left, right], axis=1))
    features = jnp.concatenate(pieces, axis=1)
    return jnp.concatenate([features, jnp.zeros_like(features)], axis=0).astype(BF16)


def split(value):
    high = value.astype(BF16)
    low = (value - high.astype(F32)).astype(BF16)
    return high, low


def interfere_kernel(first, place_ref, sent_ref, heard_ref, *rest):
    if first:
        total_ref, high_ref, low_ref = rest
    else:
        _, before_ref, total_ref, high_ref, low_ref = rest
    x, y, z0, z2, z1, zhi, core = (place_ref[i] for i in range(7))
    source_core = core if first else 1 - core
    senders = spread(sent_ref, BLOCK, lambda k: k)
    listeners = spread(heard_ref, 0, lambda k: (((k & 3) ^ y) << 2) | ((k >> 2) ^ x))
    powers = sent_ref[:, 0:BLOCK, :].reshape(HALF, BANDS)
    power_high, power_low = split(powers)
    power_both = jnp.concatenate([power_high, power_low], axis=1)
    tile_rows, tile_cols = 256, 128
    receiver_base = (z2 * 4 + z1 * 2 + z0) * 4096 + zhi * 128 + core * 64
    sender_base = y * 8192 + source_core * 2048 + x * 64
    for r in range(0, ROWS, tile_rows):
        row = lax.broadcasted_iota(jnp.int32, (tile_rows, tile_cols), 0) + r
        block = row >> 6
        row_id = receiver_base + (block >> 2) * 1024 + (block & 3) * 256 + (row & 63)
        for c in range(0, HALF, tile_cols):
            col = lax.broadcasted_iota(jnp.int32, (1, tile_cols), 1) + c
            zed = col >> 6
            zlo = ((zed >> 1) & 1) * 4 + (zed & 1) * 2 + (zed >> 3)
            col_id = sender_base + ((zed >> 2) & 1) * 4096 + zlo * 256 + (col & 63)
            square = lax.dot_general(
                listeners[:, r : r + tile_rows],
                senders[:, c : c + tile_cols],
                (((0,), (0,)), ((), ())),
                preferred_element_type=F32,
            )
            guess = pl.reciprocal(square, approx=True)
            gain = guess * (2.0 - square * guess)
            gain = jnp.where(row_id == col_id, 0.0, gain)
            high, low = split(gain)
            side, at = c // WIDE, c % WIDE
            high_ref[side, r : r + tile_rows, at : at + tile_cols] = high
            low_ref[side, r : r + tile_rows, at : at + tile_cols] = low
        product = jnp.zeros((tile_rows, 2 * BANDS), F32)
        for side in (0, 1):
            right = power_both[side * WIDE : (side + 1) * WIDE, :]
            for gain_ref in (high_ref, low_ref):
                left = gain_ref[side, r : r + tile_rows, :]
                product = product + jnp.dot(left, right, preferred_element_type=F32)
        part = product[:, :BANDS] + product[:, BANDS:]
        if not first:
            part = part + before_ref[r : r + tile_rows, :]
        total_ref[r : r + tile_rows, :] = part


def turn_kernel(pressure_ref, both_ref):
    pressure = pressure_ref[...].reshape(ROWS, BANDS).T
    pressure_high, pressure_low = split(pressure)
    both_ref[0:BANDS, :] = pressure_high
    both_ref[BANDS:, :] = pressure_low


def react_kernel(place_ref, both_ref, high_ref, low_ref, pushed_ref):
    both = both_ref[...]
    step = 256
    for k in (0, 1):
        side = place_ref[2] ^ k
        for c in range(0, WIDE, step):
            product = jnp.dot(both, high_ref[side, :, c : c + step], preferred_element_type=F32)
            product = product + jnp.dot(
                both, low_ref[side, :, c : c + step], preferred_element_type=F32
            )
            pushed_ref[k, c : c + step, :] = (product[:BANDS, :] + product[BANDS:, :]).T


def join_kernel(a_ref, b_ref, out_ref):
    rows = a_ref.shape[0]
    out_ref[0:rows, :] = a_ref[...]
    out_ref[rows:, :] = b_ref[...]


def join(a, b):
    rows, lanes = a.shape
    return call(join_kernel, shape(2 * rows, lanes), 2, 0, 16 * a.size)(a, b)


def combine_kernel(a_ref, b_ref, kept_ref, passed_ref):
    kept_ref[...] = a_ref[0] + b_ref[0]
    passed_ref[...] = a_ref[1] + b_ref[1]


def add_kernel(a_ref, b_ref, sum_ref):
    sum_ref[...] = a_ref[...] + b_ref[...]


def add_blocks(ref, count):
    total = ref[0, 0:BLOCK, :]
    for k in range(1, count):
        total = total + ref[k, 0:BLOCK, :]
    return total


def derive_kernel(
    parts_ref, mine_ref, listener_ref, weight_ref, fair_ref, quality_ref, own_ref, pressure_ref
):
    interference = add_blocks(parts_ref, NXY)
    powers = mine_ref[0:BLOCK, :]
    dx = listener_ref[0:1, :].astype(F32) + 0.5 * mine_ref[BLOCK : BLOCK + 1, 0:BLOCK]
    dy = listener_ref[1:2, :].astype(F32) + 0.5 * mine_ref[BLOCK + 1 : BLOCK + 2, 0:BLOCK]
    own_gain = 1.0 / (1.0 + dx * dx + dy * dy)
    weight = WEIGHT_UNIT * weight_ref[...].astype(F32)
    fair = fair_ref[...].astype(F32)
    rows = jnp.concatenate([own_gain, weight, fair, jnp.zeros((5, BLOCK), F32)], axis=0)
    rows = jnp.concatenate([rows, jnp.zeros_like(rows)], axis=1)
    columns = jnp.concatenate([rows, jnp.zeros((120, 128), F32)], axis=0).T
    own_gain = columns[0:BLOCK, 0:1]
    weight = columns[0:BLOCK, 1:2]
    fair = columns[0:BLOCK, 2:3]
    signal = ARRAY_GAIN * own_gain * powers
    denominator = NOISE_POWER + interference
    quality = signal / denominator
    marginal = weight * jnp.exp(-fair * jnp.log(quality)) / denominator
    quality_ref[...] = quality
    own_ref[...] = ARRAY_GAIN * own_gain * marginal
    pressure = marginal * quality
    for k in range(NXY):
        pressure_ref[k] = pressure


def finish_kernel(step_ref, parts_ref, own_ref, powers_ref, gradient_ref, power_ref, gap_ref):
    gradient = own_ref[...] - add_blocks(parts_ref, NZ // 2)
    powers = powers_ref[...]
    target = PEAK_POWER * jax.nn.sigmoid(gradient)
    step_size = step_ref[0].astype(F32) / 4096.0
    gradient_ref[...] = gradient
    power_ref[...] = powers + step_size * (target - powers)
    gap = PEAK_POWER * jnp.maximum(gradient, 0.0) - gradient * powers
    gap = jnp.sum(gap, axis=0, keepdims=True)
    for k in range(2 * NZ):
        gap_ref[k] = gap


def share(value, axes, count):
    return lax.all_to_all(jnp.broadcast_to(value[None], (count, *value.shape)), axes, 0, 0)


def per_device(sender_xy, listener_xy, powers, weight, fairness, step_code):
    place = jnp.stack([lax.axis_index(name).astype(jnp.int32) for name in PLACE])
    to_sender = [(b, (b % 32) * 16 + b // 32) for b in range(512)]
    to_receiver = [(s, b) for b, s in to_sender]
    swap = [(0, 1), (1, 0)]
    block, blocks = shape(BLOCK, BANDS), shape(NXY, BLOCK, BANDS)

    rows = [sender_xy, listener_xy, jnp.zeros((4, BLOCK), jnp.int32)]
    sent, heard, mine = call(
        pack_kernel, (shape(NZ, SENT, BANDS), shape(8, 128), shape(SENT, BANDS)), 2
    )(jnp.concatenate(rows, axis=0), powers)
    near = lax.all_to_all(sent, Z, 0, 0)
    for axis in XY:
        for bit in (1, 2):
            other = lax.ppermute(heard, axis, [(i, i ^ bit) for i in range(4)])
            heard = join(heard, other)
    near, heard, mine = lax.optimization_barrier((near, heard, mine))
    listeners = heard.reshape(NXY, 8, 128)
    far = lax.ppermute(near, "core", swap)
    mine = lax.ppermute(mine, AXES, to_receiver)

    gains = shape(2, ROWS, WIDE, dtype=BF16)
    work = dict(flops=2 * ROWS * HALF * 512, bytes_accessed=1 << 23)
    outs = (shape(ROWS, BANDS), gains, gains)
    part, near_high, near_low = call(
        lambda *refs: interfere_kernel(True, *refs), outs, 3, smem=(0,), **work
    )(place, near, listeners)
    part, far_high, far_low = call(
        lambda *refs: interfere_kernel(False, *refs), outs, 5, smem=(0,), **work
    )(place, far, listeners, mine, part)

    parts = lax.all_to_all(part.reshape(NXY, BLOCK, BANDS), XY, 0, 0)
    quality, own, pressure = call(derive_kernel, (block, block, blocks), 5)(
        parts, mine, listener_xy, weight[None], fairness[None]
    )
    pressures = lax.all_to_all(pressure, XY, 0, 0)
    both = call(turn_kernel, shape(2 * BANDS, ROWS, dtype=BF16), 1)(pressures)

    half = shape(2, WIDE, BANDS)
    react = call(react_kernel, half, 4, smem=(0,), **work)
    across = lax.ppermute(react(place, both, far_high, far_low), "core", swap)
    pushed = react(place, both, near_high, near_low)
    side = shape(WIDE, BANDS)
    kept, passed = call(combine_kernel, (side, side), 2)(pushed, across)
    passed = lax.ppermute(passed, "z0", swap)
    pushed = call(add_kernel, side, 2)(kept, passed)
    own = lax.ppermute(own, AXES, to_sender)
    parts = lax.all_to_all(pushed.reshape(NZ // 2, BLOCK, BANDS), EVEN, 0, 0)
    gradient, new_power, gap = call(
        finish_kernel, (block, block, shape(2 * NZ, 1, BANDS)), 4, smem=(0,)
    )(step_code, parts, own, powers)
    gap = jnp.sum(lax.all_to_all(gap, (*Z, "core"), 0, 0), axis=0)
    gap = lax.all_to_all(jnp.broadcast_to(gap[None], (NXY, 1, BANDS)), XY, 0, 0)
    return quality, gradient, new_power, (jnp.sum(gap) / (USERS * BANDS)).reshape(1)


def solution(mesh):
    fine = Mesh(mesh.devices.reshape(SIZES), AXES)
    rx, tx = ("z2", "z1", "z0", "x"), ("y", "zhi", "core")
    by_sender, by_receiver = (*tx, *rx), (*rx, *tx)
    return jax.shard_map(
        per_device,
        mesh=fine,
        in_specs=(
            P(None, by_sender),
            P(None, by_receiver),
            P(by_sender, None),
            P(by_receiver),
            P(by_receiver),
            P(),
        ),
        out_specs=(P(by_receiver, None), P(by_sender, None), P(by_sender, None), P()),
        check_vma=False,
    )
```

```python
import jax
import jax.numpy as jnp
from jax import lax
from jax.experimental import pallas as pl
from jax.experimental.pallas import tpu as pltpu
from jax.sharding import Mesh
from jax.sharding import PartitionSpec as P

NOISE_POWER = 0.05
ARRAY_GAIN = 32.0
WEIGHT_UNIT = 1.0 / 16.0
PEAK_POWER = 1.0

AXES = ("z2", "z1", "z0", "x", "y", "zhi", "core")
SIZES = (2, 2, 2, 4, 4, 2, 2)
EVEN = ("zhi", "z2", "z1")
Z = ("z0", *EVEN)
XY = ("x", "y")
NZ, NXY = 16, 16
BLOCK, BANDS = 64, 128
SENT = BLOCK + 8
HALF = NZ * BLOCK
WIDE = HALF // 2
ROWS = NXY * BLOCK
USERS = 32768
VMEM_LIMIT = 20 * 1024 * 1024
F32, BF16 = jnp.float32, jnp.bfloat16
PLACE = ("x", "y", "z0", "z2", "z1", "zhi", "core")


def whole():
    return pl.BlockSpec(memory_space=pltpu.VMEM)


def call(kernel, outs, n_in, flops=0, bytes_accessed=1 << 20, smem=()):
    def spec(i):
        return pl.BlockSpec(memory_space=pltpu.SMEM) if i in smem else whole()

    many = isinstance(outs, (list, tuple))
    return pl.pallas_call(
        kernel,
        out_shape=outs,
        in_specs=[spec(i) for i in range(n_in)],
        out_specs=[whole() for _ in outs] if many else whole(),
        compiler_params=pltpu.CompilerParams(vmem_limit_bytes=VMEM_LIMIT),
        cost_estimate=pl.CostEstimate(flops=flops, bytes_accessed=bytes_accessed, transcendentals=0),
    )


def shape(*dims, dtype=F32):
    return jax.ShapeDtypeStruct(dims, dtype)


def split_norm(norm):
    low = norm & 511
    odd = low & 1
    return norm - low, low - odd, odd


def hear_kernel(info_ref, heard_ref):
    lx, ly = info_ref[0:1, :], info_ref[1:2, :]
    one = jnp.ones_like(lx)
    l1, l2, l3 = split_norm(lx * lx + ly * ly + 1)
    heard = jnp.concatenate([lx, ly, l1, l2, l3, one, one, one], axis=0).astype(F32)
    user = jnp.concatenate([info_ref[2:4, :].astype(F32), jnp.zeros((6, BLOCK), F32)], axis=0)
    heard_ref[...] = jnp.concatenate([heard, user], axis=1)


def pack_kernel(sender_ref, powers_ref, sent_ref):
    sx, sy = sender_ref[0:1, :], sender_ref[1:2, :]
    one = jnp.ones_like(sx)
    s1, s2, s3 = split_norm(sx * sx + sy * sy)
    sent = jnp.concatenate([-2 * sx, -2 * sy, one, one, one, s1, s2, s3], axis=0).astype(F32)
    sent = jnp.concatenate([sent, jnp.zeros_like(sent)], axis=1)
    powers = powers_ref[...]
    for k in range(NZ):
        sent_ref[k, 0:BLOCK, :] = powers
        sent_ref[k, BLOCK:SENT, :] = sent


def spread(parts, row, index):
    pieces = []
    for k in range(0, 16, 2):
        left = parts[index(k), row : row + 8, 0:BLOCK]
        right = parts[index(k + 1), row : row + 8, 0:BLOCK]
        pieces.append(jnp.concatenate([left, right], axis=1))
    features = jnp.concatenate(pieces, axis=1)
    return jnp.concatenate([features, jnp.zeros_like(features)], axis=0).astype(BF16)


def split(value):
    high = value.astype(BF16)
    low = (value - high.astype(F32)).astype(BF16)
    return high, low


def interfere_kernel(first, place_ref, sent_ref, heard_ref, *rest):
    if first:
        total_ref, high_ref, low_ref = rest
    else:
        before_ref, total_ref, high_ref, low_ref = rest
    x, y, z0, z2, z1, zhi, core = (place_ref[i] for i in range(7))
    source_core = core if first else 1 - core
    senders = spread(sent_ref, BLOCK, lambda k: k)
    listeners = spread(heard_ref, 0, lambda k: (((k & 3) ^ y) << 2) | ((k >> 2) ^ x))
    powers = sent_ref[:, 0:BLOCK, :].reshape(HALF, BANDS)
    power_high, power_low = split(powers)
    power_both = jnp.concatenate([power_high, power_low], axis=1)
    tile_rows, tile_cols = 256, 128
    receiver_base = zhi * 4096 + core * 2048 + (z2 * 4 + z1 * 2 + z0) * 256
    sender_base = y * 8192 + source_core * 2048 + x * 64
    for r in range(0, ROWS, tile_rows):
        row = lax.broadcasted_iota(jnp.int32, (tile_rows, tile_cols), 0) + r
        block = row >> 6
        row_id = receiver_base + (block & 3) * 8192 + (block >> 2) * 64 + (row & 63)
        for c in range(0, HALF, tile_cols):
            col = lax.broadcasted_iota(jnp.int32, (1, tile_cols), 1) + c
            zed = col >> 6
            zlo = ((zed >> 1) & 1) * 4 + (zed & 1) * 2 + (zed >> 3)
            col_id = sender_base + ((zed >> 2) & 1) * 4096 + zlo * 256 + (col & 63)
            square = lax.dot_general(
                listeners[:, r : r + tile_rows],
                senders[:, c : c + tile_cols],
                (((0,), (0,)), ((), ())),
                preferred_element_type=F32,
            )
            guess = pl.reciprocal(square, approx=True)
            gain = guess * (2.0 - square * guess)
            gain = jnp.where(row_id == col_id, 0.0, gain)
            high, low = split(gain)
            side, at = c // WIDE, c % WIDE
            high_ref[side, r : r + tile_rows, at : at + tile_cols] = high
            low_ref[side, r : r + tile_rows, at : at + tile_cols] = low
        product = jnp.zeros((tile_rows, 2 * BANDS), F32)
        for side in (0, 1):
            right = power_both[side * WIDE : (side + 1) * WIDE, :]
            for gain_ref in (high_ref, low_ref):
                left = gain_ref[side, r : r + tile_rows, :]
                product = product + jnp.dot(left, right, preferred_element_type=F32)
        part = product[:, :BANDS] + product[:, BANDS:]
        if not first:
            part = part + before_ref[r : r + tile_rows, :]
        total_ref[r : r + tile_rows, :] = part


def turn_kernel(pressure_ref, both_ref):
    pressure = pressure_ref[...].reshape(ROWS, BANDS).T
    pressure_high, pressure_low = split(pressure)
    both_ref[0:BANDS, :] = pressure_high
    both_ref[BANDS:, :] = pressure_low


def react_kernel(sides, place_ref, both_ref, high_ref, low_ref, pushed_ref):
    both = both_ref[...]
    step = 256
    for k, flip in enumerate(sides):
        side = place_ref[2] ^ flip
        for c in range(0, WIDE, step):
            product = jnp.dot(both, high_ref[side, :, c : c + step], preferred_element_type=F32)
            product = product + jnp.dot(
                both, low_ref[side, :, c : c + step], preferred_element_type=F32
            )
            pushed_ref[k, c : c + step, :] = (product[:BANDS, :] + product[BANDS:, :]).T


def join_kernel(a_ref, b_ref, out_ref):
    rows = a_ref.shape[0]
    out_ref[0:rows, :] = a_ref[...]
    out_ref[rows:, :] = b_ref[...]


def join(a, b):
    rows, lanes = a.shape
    return call(join_kernel, shape(2 * rows, lanes), 2, 0, 16 * a.size)(a, b)


def add_kernel(side, near_ref, across_ref, *rest):
    total = near_ref[0] + across_ref[side]
    for ref in rest[:-1]:
        total = total + ref[...]
    rest[-1][...] = total


def add(side, *parts):
    def kernel(*refs):
        add_kernel(side, *refs)

    size = WIDE * BANDS
    return call(kernel, shape(WIDE, BANDS), len(parts), size, 12 * size)(*parts)


def fold_kernel(parts_ref, out_ref):
    total = jnp.sum(parts_ref[...], axis=0)
    for k in range(NXY):
        out_ref[k] = total


def add_blocks(ref, count):
    total = ref[0, 0:BLOCK, :]
    for k in range(1, count):
        total = total + ref[k, 0:BLOCK, :]
    return total


def derive_kernel(
    parts_ref, powers_ref, sender_ref, heard_ref, quality_ref, own_ref, pressure_ref
):
    interference = add_blocks(parts_ref, NXY)
    powers = powers_ref[...]
    dx = heard_ref[0:1, 0:BLOCK] - sender_ref[0:1, :].astype(F32)
    dy = heard_ref[1:2, 0:BLOCK] - sender_ref[1:2, :].astype(F32)
    own_gain = 1.0 / (1.0 + dx * dx + dy * dy)
    weight = WEIGHT_UNIT * heard_ref[0:1, BLOCK:]
    fair = heard_ref[1:2, BLOCK:]
    rows = jnp.concatenate([own_gain, weight, fair, jnp.zeros((5, BLOCK), F32)], axis=0)
    rows = jnp.concatenate([rows, jnp.zeros_like(rows)], axis=1)
    columns = jnp.concatenate([rows, jnp.zeros((120, 128), F32)], axis=0).T
    own_gain = columns[0:BLOCK, 0:1]
    weight = columns[0:BLOCK, 1:2]
    fair = columns[0:BLOCK, 2:3]
    signal = ARRAY_GAIN * own_gain * powers
    denominator = NOISE_POWER + interference
    quality = signal / denominator
    marginal = weight * jnp.exp(-fair * jnp.log(quality)) / denominator
    quality_ref[...] = quality
    own_ref[...] = ARRAY_GAIN * own_gain * marginal
    pressure = marginal * quality
    for k in range(NXY):
        pressure_ref[k] = pressure


def finish_kernel(step_ref, parts_ref, own_ref, powers_ref, gradient_ref, power_ref, gap_ref):
    gradient = own_ref[...] - add_blocks(parts_ref, NZ // 2)
    powers = powers_ref[...]
    target = PEAK_POWER * jax.nn.sigmoid(gradient)
    step_size = step_ref[0].astype(F32) / 4096.0
    gradient_ref[...] = gradient
    power_ref[...] = powers + step_size * (target - powers)
    gap = PEAK_POWER * jnp.maximum(gradient, 0.0) - gradient * powers
    gap = jnp.sum(gap, axis=0, keepdims=True)
    for k in range(2 * NZ):
        gap_ref[k] = gap


def share(value, axes, count):
    return lax.all_to_all(jnp.broadcast_to(value[None], (count, *value.shape)), axes, 0, 0)


def per_device(sender_xy, listener_xy, powers, weight, fairness, step_code):
    place = jnp.stack([lax.axis_index(name).astype(jnp.int32) for name in PLACE])
    to_sender = [(b, (b % 32) * 16 + b // 32) for b in range(512)]
    to_receiver = [(s, b) for b, s in to_sender]
    swap = [(0, 1), (1, 0)]
    block, blocks = shape(BLOCK, BANDS), shape(NXY, BLOCK, BANDS)

    rows = [listener_xy, weight[None], fairness[None]]
    heard = call(hear_kernel, shape(8, 128), 1)(jnp.concatenate(rows, axis=0))
    heard = lax.ppermute(heard, AXES, to_sender)
    sent = call(pack_kernel, shape(NZ, SENT, BANDS), 2)(sender_xy, powers)
    heard, sent = lax.optimization_barrier((heard, sent))
    mine = heard
    near = lax.all_to_all(sent, Z, 0, 0)
    for axis in XY:
        for bit in (1, 2):
            other = lax.ppermute(heard, axis, [(i, i ^ bit) for i in range(4)])
            heard = join(heard, other)
    near, heard = lax.optimization_barrier((near, heard))
    listeners = heard.reshape(NXY, 8, 128)
    far = lax.ppermute(near, "core", swap)

    gains = shape(2, ROWS, WIDE, dtype=BF16)
    work = dict(flops=2 * ROWS * HALF * 512, bytes_accessed=1 << 23)
    outs = (shape(ROWS, BANDS), gains, gains)
    part, near_high, near_low = call(
        lambda *refs: interfere_kernel(True, *refs), outs, 3, smem=(0,), **work
    )(place, near, listeners)
    part, far_high, far_low = call(
        lambda *refs: interfere_kernel(False, *refs), outs, 4, smem=(0,), **work
    )(place, far, listeners, part)

    parts = lax.all_to_all(part.reshape(NXY, BLOCK, BANDS), XY, 0, 0)
    quality, own, pressure = call(derive_kernel, (block, block, blocks), 4)(
        parts, powers, sender_xy, mine
    )
    pressures = lax.all_to_all(pressure, XY, 0, 0)
    both = call(turn_kernel, shape(2 * BANDS, ROWS, dtype=BF16), 1)(pressures)

    def react(high, low, *sides):
        def kernel(*refs):
            react_kernel(sides, *refs)

        cost = dict(flops=len(sides) * work["flops"] // 2, bytes_accessed=len(sides) << 21)
        out = shape(len(sides), WIDE, BANDS)
        return call(kernel, out, 4, smem=(0,), **cost)(place, both, high, low)

    across = lax.ppermute(react(far_high, far_low, 0, 1), "core", swap)
    passed = add(1, react(near_high, near_low, 1), across)
    passed = lax.ppermute(passed, "z0", swap)
    pushed = add(0, react(near_high, near_low, 0), across, passed)
    quality = lax.ppermute(quality, AXES, to_receiver)
    parts = lax.all_to_all(pushed.reshape(NZ // 2, BLOCK, BANDS), EVEN, 0, 0)
    gradient, new_power, gap = call(
        finish_kernel, (block, block, shape(2 * NZ, 1, BANDS)), 4, smem=(0,)
    )(step_code, parts, own, powers)
    gap = lax.all_to_all(gap, (*Z, "core"), 0, 0)
    gap = call(fold_kernel, shape(NXY, 1, BANDS), 1)(gap)
    gap = lax.all_to_all(gap, XY, 0, 0)
    return quality, gradient, new_power, (jnp.sum(gap) / (USERS * BANDS)).reshape(1)


def solution(mesh):
    fine = Mesh(mesh.devices.reshape(SIZES), AXES)
    rx, tx = ("z2", "z1", "z0", "x"), ("y", "zhi", "core")
    by_sender, by_receiver = (*tx, *rx), (*rx, *tx)
    return jax.shard_map(
        per_device,
        mesh=fine,
        in_specs=(
            P(None, by_sender),
            P(None, by_receiver),
            P(by_sender, None),
            P(by_receiver),
            P(by_receiver),
            P(),
        ),
        out_specs=(P(by_receiver, None), P(by_sender, None), P(by_sender, None), P()),
        check_vma=False,
    )
```

```python
import jax
import jax.numpy as jnp
from jax import lax
from jax.experimental import pallas as pl
from jax.experimental.pallas import tpu as pltpu
from jax.sharding import Mesh
from jax.sharding import PartitionSpec as P

NOISE_POWER = 0.05
ARRAY_GAIN = 32.0
WEIGHT_UNIT = 1.0 / 16.0
PEAK_POWER = 1.0

AXES = ("z2", "z1", "z0", "x", "y", "zhi", "core")
SIZES = (2, 2, 2, 4, 4, 2, 2)
EVEN = ("zhi", "z2", "z1")
Z = (*EVEN, "z0")
XY = ("x", "y")
NZ, NXY = 16, 16
BLOCK, BANDS = 64, 128
SENT = BLOCK + 8
HALF = NZ * BLOCK
WIDE = HALF // 2
ROWS = NXY * BLOCK
USERS = 32768
VMEM_LIMIT = 20 * 1024 * 1024
F32, BF16 = jnp.float32, jnp.bfloat16
PLACE = ("x", "y", "z0", "z2", "z1", "zhi", "core")


def whole():
    return pl.BlockSpec(memory_space=pltpu.VMEM)


def call(kernel, outs, n_in, flops=0, bytes_accessed=1 << 20, smem=()):
    def spec(i):
        return pl.BlockSpec(memory_space=pltpu.SMEM) if i in smem else whole()

    many = isinstance(outs, (list, tuple))
    return pl.pallas_call(
        kernel,
        out_shape=outs,
        in_specs=[spec(i) for i in range(n_in)],
        out_specs=[whole() for _ in outs] if many else whole(),
        compiler_params=pltpu.CompilerParams(vmem_limit_bytes=VMEM_LIMIT),
        cost_estimate=pl.CostEstimate(flops=flops, bytes_accessed=bytes_accessed, transcendentals=0),
    )


def shape(*dims, dtype=F32):
    return jax.ShapeDtypeStruct(dims, dtype)


def split_norm(norm):
    low = norm & 511
    odd = low & 1
    return norm - low, low - odd, odd


def pack_kernel(info_ref, powers_ref, sent_ref, heard_ref):
    sx, sy, lx, ly = (info_ref[i : i + 1, :] for i in range(4))
    one = jnp.ones_like(sx)
    s1, s2, s3 = split_norm(sx * sx + sy * sy)
    l1, l2, l3 = split_norm(lx * lx + ly * ly + 1)
    sent = jnp.concatenate([-2 * sx, -2 * sy, one, one, one, s1, s2, s3], axis=0).astype(F32)
    heard = jnp.concatenate([lx, ly, l1, l2, l3, one, one, one], axis=0).astype(F32)
    pad = jnp.zeros_like(sent)
    sent_ref[0:BLOCK, :] = powers_ref[...]
    sent_ref[BLOCK:, :] = jnp.concatenate([sent, pad], axis=1)
    heard = jnp.concatenate([heard, pad], axis=1)
    for k in range(NXY):
        heard_ref[k] = heard


def spread(parts, row, index):
    pieces = []
    for k in range(0, 16, 2):
        left = parts[index(k), row : row + 8, 0:BLOCK]
        right = parts[index(k + 1), row : row + 8, 0:BLOCK]
        pieces.append(jnp.concatenate([left, right], axis=1))
    features = jnp.concatenate(pieces, axis=1)
    return jnp.concatenate([features, jnp.zeros_like(features)], axis=0).astype(BF16)


def split(value):
    high = value.astype(BF16)
    low = (value - high.astype(F32)).astype(BF16)
    return high, low


def even_first(k):
    return (k & 7) * 2 + (k >> 3)


def interfere_kernel(first, place_ref, sent_ref, heard_ref, *rest):
    if first:
        total_ref, high_ref, low_ref = rest
    else:
        near_ref, before_ref, total_ref, high_ref, low_ref = rest
    x, y, z0, z2, z1, zhi, core = (place_ref[i] for i in range(7))
    source_core = core if first else 1 - core
    senders = spread(sent_ref, BLOCK, even_first)
    listeners = spread(heard_ref, 0, lambda k: k)
    powers = jnp.concatenate([sent_ref[even_first(k), 0:BLOCK, :] for k in range(NZ)], axis=0)
    power_high, power_low = split(powers)
    power_both = jnp.concatenate([power_high, power_low], axis=1)
    tile_rows, tile_cols = 256, 128
    per_tile = tile_rows // BLOCK
    receiver_base = (z2 * 4 + z1 * 2 + z0) * 4096 + zhi * 128 + core * 64
    sender_base = y * 8192 + source_core * 2048 + x * 64
    for r in range(0, ROWS, tile_rows):
        row = lax.broadcasted_iota(jnp.int32, (tile_rows, tile_cols), 0) + r
        block = row >> 6
        row_id = receiver_base + (block >> 2) * 1024 + (block & 3) * 256 + (row & 63)
        for c in range(0, HALF, tile_cols):
            col = lax.broadcasted_iota(jnp.int32, (1, tile_cols), 1) + c
            zed = even_first(col >> 6)
            col_id = sender_base + (zed >> 3) * 4096 + (zed & 7) * 256 + (col & 63)
            square = lax.dot_general(
                listeners[:, r : r + tile_rows],
                senders[:, c : c + tile_cols],
                (((0,), (0,)), ((), ())),
                preferred_element_type=F32,
            )
            guess = pl.reciprocal(square, approx=True)
            gain = guess * (2.0 - square * guess)
            gain = jnp.where(row_id == col_id, 0.0, gain)
            high, low = split(gain)
            side, at = c // WIDE, c % WIDE
            high_ref[side, r : r + tile_rows, at : at + tile_cols] = high
            low_ref[side, r : r + tile_rows, at : at + tile_cols] = low
        product = jnp.zeros((tile_rows, 2 * BANDS), F32)
        for side in (0, 1):
            right = power_both[side * WIDE : (side + 1) * WIDE, :]
            for gain_ref in (high_ref, low_ref):
                left = gain_ref[side, r : r + tile_rows, :]
                product = product + jnp.dot(left, right, preferred_element_type=F32)
        part = product[:, :BANDS] + product[:, BANDS:]
        if first:
            total_ref[r : r + tile_rows, :] = part
        else:
            k = r // BLOCK
            part = part + before_ref[r : r + tile_rows, :]
            total_ref[k : k + per_tile, 0:BLOCK, :] = part.reshape(per_tile, BLOCK, BANDS)
    if not first:
        for k in range(NXY):
            there_x, there_y = k >> 2, k & 3
            at = z0 * 8 + (there_x & 1) * 4 + there_y
            total_ref[k, BLOCK:, :] = jnp.where(core == there_x >> 1, near_ref[at], sent_ref[at])


def turn_kernel(pressure_ref, both_ref):
    pressure = pressure_ref[...].reshape(ROWS, BANDS).T
    pressure_high, pressure_low = split(pressure)
    both_ref[0:BANDS, :] = pressure_high
    both_ref[BANDS:, :] = pressure_low


def react_kernel(sides, place_ref, both_ref, high_ref, low_ref, pushed_ref):
    both = both_ref[...]
    step = 256
    for k, flip in enumerate(sides):
        side = place_ref[2] ^ flip
        for c in range(0, WIDE, step):
            product = jnp.dot(both, high_ref[side, :, c : c + step], preferred_element_type=F32)
            product = product + jnp.dot(
                both, low_ref[side, :, c : c + step], preferred_element_type=F32
            )
            pushed_ref[k, c : c + step, :] = (product[:BANDS, :] + product[BANDS:, :]).T


def add_kernel(side, near_ref, across_ref, *rest):
    total = near_ref[0] + across_ref[side]
    for ref in rest[:-1]:
        total = total + ref[...]
    rest[-1][...] = total


def add(side, *parts):
    def kernel(*refs):
        add_kernel(side, *refs)

    size = WIDE * BANDS
    return call(kernel, shape(WIDE, BANDS), len(parts), size, 12 * size)(*parts)


def fold_kernel(parts_ref, out_ref):
    total = jnp.sum(parts_ref[...], axis=0)
    for k in range(NXY):
        out_ref[k] = total


def add_blocks(ref, count):
    total = ref[0, 0:BLOCK, :]
    for k in range(1, count):
        total = total + ref[k, 0:BLOCK, :]
    return total


def derive_kernel(
    place_ref, parts_ref, listener_ref, weight_ref, fair_ref, quality_ref, own_ref, pressure_ref
):
    interference = add_blocks(parts_ref, NXY)
    z2, z1, zhi, core = (place_ref[i] for i in range(3, 7))
    source = (zhi * 2 + core) * 4 + z2 * 2 + z1
    powers = parts_ref[source, BLOCK : 2 * BLOCK, :]
    sender = -0.5 * parts_ref[source, 2 * BLOCK :, :]
    dx = listener_ref[0:1, :].astype(F32) - sender[0:1, 0:BLOCK]
    dy = listener_ref[1:2, :].astype(F32) - sender[1:2, 0:BLOCK]
    own_gain = 1.0 / (1.0 + dx * dx + dy * dy)
    weight = WEIGHT_UNIT * weight_ref[...].astype(F32)
    fair = fair_ref[...].astype(F32)
    rows = jnp.concatenate([own_gain, weight, fair, jnp.zeros((5, BLOCK), F32)], axis=0)
    rows = jnp.concatenate([rows, jnp.zeros_like(rows)], axis=1)
    columns = jnp.concatenate([rows, jnp.zeros((120, 128), F32)], axis=0).T
    own_gain = columns[0:BLOCK, 0:1]
    weight = columns[0:BLOCK, 1:2]
    fair = columns[0:BLOCK, 2:3]
    signal = ARRAY_GAIN * own_gain * powers
    denominator = NOISE_POWER + interference
    quality = signal / denominator
    marginal = weight * jnp.exp(-fair * jnp.log(quality)) / denominator
    quality_ref[...] = quality
    own_ref[...] = ARRAY_GAIN * own_gain * marginal
    pressure = marginal * quality
    for k in range(NXY):
        pressure_ref[k] = pressure


def finish_kernel(step_ref, parts_ref, own_ref, powers_ref, gradient_ref, power_ref, gap_ref):
    gradient = own_ref[...] - add_blocks(parts_ref, NZ // 2)
    powers = powers_ref[...]
    target = PEAK_POWER * jax.nn.sigmoid(gradient)
    step_size = step_ref[0].astype(F32) / 4096.0
    gradient_ref[...] = gradient
    power_ref[...] = powers + step_size * (target - powers)
    gap = PEAK_POWER * jnp.maximum(gradient, 0.0) - gradient * powers
    gap = jnp.sum(gap, axis=0, keepdims=True)
    for k in range(2 * NZ):
        gap_ref[k] = gap


def share(value, axes, count):
    return lax.all_to_all(jnp.broadcast_to(value[None], (count, *value.shape)), axes, 0, 0)


def per_device(sender_xy, listener_xy, powers, weight, fairness, step_code):
    place = jnp.stack([lax.axis_index(name).astype(jnp.int32) for name in PLACE])
    to_sender = [(b, (b % 32) * 16 + b // 32) for b in range(512)]
    swap = [(0, 1), (1, 0)]
    block, blocks = shape(BLOCK, BANDS), shape(NXY, BLOCK, BANDS)

    sent, heard = call(pack_kernel, (shape(SENT, BANDS), shape(NXY, 8, 128)), 2)(
        jnp.concatenate([sender_xy, listener_xy], axis=0), powers
    )
    near = lax.all_gather(sent, Z, axis=0)
    listeners = lax.all_to_all(heard, XY, 0, 0)
    near, listeners = lax.optimization_barrier((near, listeners))
    far = lax.ppermute(near, "core", swap)

    gains = shape(2, ROWS, WIDE, dtype=BF16)
    work = dict(flops=2 * ROWS * HALF * 512, bytes_accessed=1 << 23)
    outs = (shape(ROWS, BANDS), gains, gains)
    part, near_high, near_low = call(
        lambda *refs: interfere_kernel(True, *refs), outs, 3, smem=(0,), **work
    )(place, near, listeners)
    part, far_high, far_low = call(
        lambda *refs: interfere_kernel(False, *refs),
        (shape(NXY, BLOCK + SENT, BANDS), gains, gains),
        5,
        smem=(0,),
        **work,
    )(place, far, listeners, near, part)

    parts = lax.all_to_all(part, XY, 0, 0)
    quality, own, pressure = call(derive_kernel, (block, block, blocks), 5, smem=(0,))(
        place, parts, listener_xy, weight[None], fairness[None]
    )
    pressures = lax.all_to_all(pressure, XY, 0, 0)
    both = call(turn_kernel, shape(2 * BANDS, ROWS, dtype=BF16), 1)(pressures)

    def react(high, low, *sides):
        def kernel(*refs):
            react_kernel(sides, *refs)

        cost = dict(flops=len(sides) * work["flops"] // 2, bytes_accessed=len(sides) << 21)
        out = shape(len(sides), WIDE, BANDS)
        return call(kernel, out, 4, smem=(0,), **cost)(place, both, high, low)

    across = lax.ppermute(react(far_high, far_low, 0, 1), "core", swap)
    passed = add(1, react(near_high, near_low, 1), across)
    passed = lax.ppermute(passed, "z0", swap)
    pushed = add(0, react(near_high, near_low, 0), across, passed)
    own = lax.ppermute(own, AXES, to_sender)
    parts = lax.all_to_all(pushed.reshape(NZ // 2, BLOCK, BANDS), EVEN, 0, 0)
    gradient, new_power, gap = call(
        finish_kernel, (block, block, shape(2 * NZ, 1, BANDS)), 4, smem=(0,)
    )(step_code, parts, own, powers)
    gap = lax.all_to_all(gap, (*Z, "core"), 0, 0)
    gap = call(fold_kernel, shape(NXY, 1, BANDS), 1)(gap)
    gap = lax.all_to_all(gap, XY, 0, 0)
    return quality, gradient, new_power, (jnp.sum(gap) / (USERS * BANDS)).reshape(1)


def solution(mesh):
    fine = Mesh(mesh.devices.reshape(SIZES), AXES)
    rx, tx = ("z2", "z1", "z0", "x"), ("y", "zhi", "core")
    by_sender, by_receiver = (*tx, *rx), (*rx, *tx)
    return jax.shard_map(
        per_device,
        mesh=fine,
        in_specs=(
            P(None, by_sender),
            P(None, by_receiver),
            P(by_sender, None),
            P(by_receiver),
            P(by_receiver),
            P(),
        ),
        out_specs=(P(by_receiver, None), P(by_sender, None), P(by_sender, None), P()),
        check_vma=False,
    )
```

```python
import jax
import jax.numpy as jnp
from jax import lax
from jax.experimental import pallas as pl
from jax.experimental.pallas import tpu as pltpu
from jax.sharding import Mesh
from jax.sharding import PartitionSpec as P

NOISE_POWER = 0.05
ARRAY_GAIN = 32.0
WEIGHT_UNIT = 1.0 / 16.0
PEAK_POWER = 1.0

AXES = ("z2", "z1", "z0", "x", "y", "zhi", "core")
SIZES = (2, 2, 2, 4, 4, 2, 2)
Z = ("zhi", "z2", "z1", "z0")
XY = ("x", "y")
PLACE = ("x", "y", "z0", "z2", "z1", "zhi", "core")
NZ, NXY = 16, 16
BLOCK, BANDS = 64, 128
SENT = BLOCK + 8
HALF = NZ * BLOCK
ROWS = NXY * BLOCK
USERS = 32768
VMEM_LIMIT = 20 * 1024 * 1024
F32, BF16 = jnp.float32, jnp.bfloat16


def whole():
    return pl.BlockSpec(memory_space=pltpu.VMEM)


def call(kernel, outs, n_in, flops=0, bytes_accessed=1 << 20, smem=()):
    def spec(i):
        return pl.BlockSpec(memory_space=pltpu.SMEM) if i in smem else whole()

    many = isinstance(outs, (list, tuple))
    return pl.pallas_call(
        kernel,
        out_shape=outs,
        in_specs=[spec(i) for i in range(n_in)],
        out_specs=[whole() for _ in outs] if many else whole(),
        compiler_params=pltpu.CompilerParams(vmem_limit_bytes=VMEM_LIMIT),
        cost_estimate=pl.CostEstimate(flops=flops, bytes_accessed=bytes_accessed, transcendentals=0),
    )


def shape(*dims, dtype=F32):
    return jax.ShapeDtypeStruct(dims, dtype)


def split_norm(norm):
    low = norm & 511
    odd = low & 1
    return norm - low, low - odd, odd


def hear_kernel(info_ref, heard_ref):
    lx, ly = info_ref[0:1, :], info_ref[1:2, :]
    one = jnp.ones_like(lx)
    l1, l2, l3 = split_norm(lx * lx + ly * ly + 1)
    heard = jnp.concatenate([lx, ly, l1, l2, l3, one, one, one], axis=0).astype(F32)
    user = jnp.concatenate([info_ref[2:4, :].astype(F32), jnp.zeros((6, BLOCK), F32)], axis=0)
    heard_ref[...] = jnp.concatenate([heard, user], axis=1)


def pack_kernel(sender_ref, powers_ref, sent_ref):
    sx, sy = sender_ref[0:1, :], sender_ref[1:2, :]
    one = jnp.ones_like(sx)
    s1, s2, s3 = split_norm(sx * sx + sy * sy)
    sent = jnp.concatenate([-2 * sx, -2 * sy, one, one, one, s1, s2, s3], axis=0).astype(F32)
    sent_ref[0:BLOCK, :] = powers_ref[...]
    sent_ref[BLOCK:, :] = jnp.concatenate([sent, jnp.zeros_like(sent)], axis=1)


def plane_kernel(heard_ref, sent_ref, plane_ref):
    both = jnp.concatenate([heard_ref[:, 0:BLOCK], sent_ref[BLOCK:, 0:BLOCK]], axis=1)
    for k in range(NXY):
        plane_ref[k] = both


def spread(parts, row, lane):
    pieces = []
    for k in range(0, 16, 2):
        left = parts[k, row : row + 8, lane : lane + BLOCK]
        right = parts[k + 1, row : row + 8, lane : lane + BLOCK]
        pieces.append(jnp.concatenate([left, right], axis=1))
    features = jnp.concatenate(pieces, axis=1)
    return jnp.concatenate([features, jnp.zeros_like(features)], axis=0).astype(BF16)


def split(value):
    high = value.astype(BF16)
    low = (value - high.astype(F32)).astype(BF16)
    return high, low


def gain_kernel(far, lane, place_ref, plane_ref, column_ref, *rest):
    *before, total_ref = rest
    x, y, z0, z2, z1, zhi, core = (place_ref[i] for i in range(7))
    rows = spread(plane_ref, 0, lane)
    columns = spread(column_ref, BLOCK, 0)
    value_high, value_low = split(column_ref[:, 0:BLOCK, :].reshape(HALF, BANDS))
    values = jnp.concatenate([value_high, value_low], axis=1)
    values = jnp.concatenate([values, values], axis=0)
    row_base = zhi * 4096 + core * 2048 + (z2 * 4 + z1 * 2 + z0) * 256
    col_base = y * 8192 + (1 - core if far else core) * 2048 + x * 64
    tile = 128
    for r in range(0, ROWS, tile):
        row = lax.broadcasted_iota(jnp.int32, (tile, tile), 0) + r
        block = row >> 6
        row_id = row_base + (block & 3) * 8192 + (block >> 2) * 64 + (row & 63)
        highs, lows = [], []
        for c in range(0, HALF, tile):
            col = lax.broadcasted_iota(jnp.int32, (1, tile), 1) + c
            zed = col >> 6
            col_id = col_base + (zed >> 3) * 4096 + (zed & 7) * 256 + (col & 63)
            square = lax.dot_general(
                rows[:, r : r + tile],
                columns[:, c : c + tile],
                (((0,), (0,)), ((), ())),
                preferred_element_type=F32,
            )
            guess = pl.reciprocal(square, approx=True)
            gain = guess * (2.0 - square * guess)
            gain = jnp.where(row_id == col_id, 0.0, gain)
            high, low = split(gain)
            highs.append(high)
            lows.append(low)
        gains = jnp.concatenate(highs + lows, axis=1)
        product = jnp.dot(gains, values, preferred_element_type=F32)
        part = product[:, :BANDS] + product[:, BANDS:]
        for ref in before:
            part = part + ref[r : r + tile, :]
        total_ref[r : r + tile, :] = part


def add_blocks(ref):
    total = ref[0]
    for k in range(1, NXY):
        total = total + ref[k]
    return total


def derive_kernel(parts_ref, powers_ref, sent_ref, heard_ref, quality_ref, own_ref, column_ref):
    interference = add_blocks(parts_ref)
    dx = heard_ref[0:1, 0:BLOCK] + 0.5 * sent_ref[BLOCK : BLOCK + 1, 0:BLOCK]
    dy = heard_ref[1:2, 0:BLOCK] + 0.5 * sent_ref[BLOCK + 1 : BLOCK + 2, 0:BLOCK]
    own_gain = 1.0 / (1.0 + dx * dx + dy * dy)
    weight = WEIGHT_UNIT * heard_ref[0:1, BLOCK:]
    fair = heard_ref[1:2, BLOCK:]
    rows = jnp.concatenate([own_gain, weight, fair, jnp.zeros((5, BLOCK), F32)], axis=0)
    rows = jnp.concatenate([rows, jnp.zeros_like(rows)], axis=1)
    columns = jnp.concatenate([rows, jnp.zeros((120, 128), F32)], axis=0).T
    own_gain = columns[0:BLOCK, 0:1]
    weight = columns[0:BLOCK, 1:2]
    fair = columns[0:BLOCK, 2:3]
    signal = ARRAY_GAIN * own_gain * powers_ref[...]
    denominator = NOISE_POWER + interference
    quality = signal / denominator
    marginal = weight * jnp.exp(-fair * jnp.log(quality)) / denominator
    quality_ref[...] = quality
    own_ref[...] = ARRAY_GAIN * own_gain * marginal
    column_ref[0:BLOCK, :] = marginal * quality
    column_ref[BLOCK:, :] = heard_ref[...]


def finish_kernel(step_ref, parts_ref, own_ref, powers_ref, gradient_ref, power_ref, gap_ref):
    gradient = own_ref[...] - add_blocks(parts_ref)
    powers = powers_ref[...]
    target = PEAK_POWER * jax.nn.sigmoid(gradient)
    step_size = step_ref[0].astype(F32) / 4096.0
    gradient_ref[...] = gradient
    power_ref[...] = powers + step_size * (target - powers)
    gap = PEAK_POWER * jnp.maximum(gradient, 0.0) - gradient * powers
    gap = jnp.sum(gap, axis=0, keepdims=True)
    for k in range(2 * NZ):
        gap_ref[k] = gap


def fold_kernel(parts_ref, out_ref):
    total = jnp.sum(parts_ref[...], axis=0)
    for k in range(NXY):
        out_ref[k] = total


def per_device(sender_xy, listener_xy, powers, weight, fairness, step_code):
    place = jnp.stack([lax.axis_index(name).astype(jnp.int32) for name in PLACE])
    to_sender = [(b, (b % 32) * 16 + b // 32) for b in range(512)]
    to_receiver = [(s, b) for b, s in to_sender]
    swap = [(0, 1), (1, 0)]
    block, product = shape(BLOCK, BANDS), shape(ROWS, BANDS)
    work = dict(flops=2 * ROWS * HALF * 512, bytes_accessed=1 << 22)

    def gain_product(far, lane, *args):
        def kernel(*refs):
            gain_kernel(far, lane, *refs)

        return call(kernel, product, 1 + len(args), smem=(0,), **work)(place, *args)

    def spread_sum(near, far, plane, lane):
        part = gain_product(False, lane, plane, near)
        part = gain_product(True, lane, plane, far, part)
        return lax.all_to_all(part.reshape(NXY, BLOCK, BANDS), XY, 0, 0)

    info = jnp.concatenate([listener_xy, weight[None], fairness[None]], axis=0)
    heard = call(hear_kernel, shape(8, 128), 1)(info)
    heard = lax.ppermute(heard, AXES, to_sender)
    sent = call(pack_kernel, shape(SENT, BANDS), 2)(sender_xy, powers)
    near = lax.all_gather(sent, Z, axis=0)
    near, heard = lax.optimization_barrier((near, heard))
    far = lax.ppermute(near, "core", swap)
    plane = call(plane_kernel, shape(NXY, 8, 128), 2)(heard, sent)
    plane = lax.all_to_all(plane, XY, 0, 0)
    parts = spread_sum(near, far, plane, 0)
    quality, own, column = call(derive_kernel, (block, block, shape(SENT, BANDS)), 4)(
        parts, powers, sent, heard
    )

    near = lax.all_gather(column, Z, axis=0)
    far = lax.ppermute(near, "core", swap)
    parts = spread_sum(near, far, plane, BLOCK)
    gradient, new_power, gap = call(
        finish_kernel, (block, block, shape(2 * NZ, 1, BANDS)), 4, smem=(0,)
    )(step_code, parts, own, powers)

    quality = lax.ppermute(quality, AXES, to_receiver)
    gap = lax.all_to_all(gap, (*Z, "core"), 0, 0)
    gap = call(fold_kernel, shape(NXY, 1, BANDS), 1)(gap)
    gap = lax.all_to_all(gap, XY, 0, 0)
    return quality, gradient, new_power, (jnp.sum(gap) / (USERS * BANDS)).reshape(1)


def solution(mesh):
    fine = Mesh(mesh.devices.reshape(SIZES), AXES)
    rx, tx = ("z2", "z1", "z0", "x"), ("y", "zhi", "core")
    by_sender, by_receiver = (*tx, *rx), (*rx, *tx)
    return jax.shard_map(
        per_device,
        mesh=fine,
        in_specs=(
            P(None, by_sender),
            P(None, by_receiver),
            P(by_sender, None),
            P(by_receiver),
            P(by_receiver),
            P(),
        ),
        out_specs=(P(by_receiver, None), P(by_sender, None), P(by_sender, None), P()),
        check_vma=False,
    )
```

```python
import jax
import jax.numpy as jnp
from jax import lax
from jax.experimental import pallas as pl
from jax.experimental.pallas import tpu as pltpu
from jax.sharding import Mesh
from jax.sharding import PartitionSpec as P

NOISE_POWER = 0.05
ARRAY_GAIN = 32.0
WEIGHT_UNIT = 1.0 / 16.0
PEAK_POWER = 1.0

AXES = ("z2", "z1", "z0", "x", "y", "zhi", "core")
SIZES = (2, 2, 2, 4, 4, 2, 2)
Z = ("zhi", "z2", "z1", "z0")
XY = ("x", "y")
PLACE = ("x", "y", "z0", "z2", "z1", "zhi", "core")
NZ, NXY = 16, 16
BLOCK, BANDS = 64, 128
SENT = BLOCK + 8
HALF = NZ * BLOCK
ROWS = NXY * BLOCK
USERS = 32768
VMEM_LIMIT = 20 * 1024 * 1024
F32, BF16 = jnp.float32, jnp.bfloat16


def whole():
    return pl.BlockSpec(memory_space=pltpu.VMEM)


def call(kernel, outs, n_in, flops=0, bytes_accessed=1 << 20, smem=()):
    def spec(i):
        return pl.BlockSpec(memory_space=pltpu.SMEM) if i in smem else whole()

    many = isinstance(outs, (list, tuple))
    return pl.pallas_call(
        kernel,
        out_shape=outs,
        in_specs=[spec(i) for i in range(n_in)],
        out_specs=[whole() for _ in outs] if many else whole(),
        compiler_params=pltpu.CompilerParams(vmem_limit_bytes=VMEM_LIMIT),
        cost_estimate=pl.CostEstimate(flops=flops, bytes_accessed=bytes_accessed, transcendentals=0),
    )


def shape(*dims, dtype=F32):
    return jax.ShapeDtypeStruct(dims, dtype)


def split_norm(norm):
    low = norm & 511
    odd = low & 1
    return norm - low, low - odd, odd


def listener_features(lx, ly):
    one = jnp.ones_like(lx)
    l1, l2, l3 = split_norm(lx * lx + ly * ly + 1)
    return jnp.concatenate([lx, ly, l1, l2, l3, one, one, one], axis=0).astype(F32)


def sender_features(sx, sy):
    one = jnp.ones_like(sx)
    s1, s2, s3 = split_norm(sx * sx + sy * sy)
    return jnp.concatenate([-2 * sx, -2 * sy, one, one, one, s1, s2, s3], axis=0).astype(F32)


def pack_kernel(info_ref, powers_ref, sent_ref):
    sent = sender_features(info_ref[0:1, :], info_ref[1:2, :])
    user = jnp.concatenate([info_ref[2:6, :].astype(F32), jnp.zeros((4, BLOCK), F32)], axis=0)
    sent_ref[0:BLOCK, :] = powers_ref[...]
    sent_ref[BLOCK:, :] = jnp.concatenate([sent, user], axis=1)


def chunk_kernel(place_ref, near_ref, far_ref, sent_ref, chunk_ref):
    zhi, core = place_ref[5], place_ref[6]
    users = []
    for k in range(NXY):
        there_x, there_y = k >> 2, k & 3
        at = (there_x >> 1) * 8 + there_y * 2 + zhi
        near, far = near_ref[at, BLOCK:, BLOCK:], far_ref[at, BLOCK:, BLOCK:]
        users.append(jnp.where(core == there_x & 1, near, far))
    places = [jnp.concatenate([user[0:1], user[1:2]], axis=1) for user in users]
    places = jnp.concatenate(places, axis=0)
    sender = -0.5 * sent_ref[BLOCK : BLOCK + 2, 0:BLOCK]
    sender = jnp.concatenate([sender[0:1], sender[1:2]], axis=1)
    for k, user in enumerate(users):
        weights = jnp.concatenate([user[2:3], user[3:4]], axis=1)
        tail = jnp.concatenate([sender, weights, jnp.zeros((6, BANDS), F32)], axis=0)
        chunk_ref[k, 0:NXY, :] = places
        chunk_ref[k, NXY:, :] = tail


def plane_kernel(place_ref, chunk_ref, listeners_ref, senders_ref, user_ref):
    x, y, z0, z2, z1, zhi, core = (place_ref[i] for i in range(7))
    source = (core * 2 + z2) * 4 + z1 * 2 + z0

    def line(pieces):
        pairs = [jnp.concatenate(pieces[k : k + 2], axis=1) for k in range(0, NXY, 2)]
        return jnp.concatenate(pairs, axis=1).astype(jnp.int32)

    def store(ref, features):
        ref[...] = jnp.concatenate([features, jnp.zeros_like(features)], axis=0).astype(BF16)

    left, right = slice(0, BLOCK), slice(BLOCK, 2 * BLOCK)
    places = chunk_ref[source, 0:NXY, :]
    lx, ly = (line([places[k : k + 1, half] for k in range(NXY)]) for half in (left, right))
    sx, sy = (line([chunk_ref[k, NXY : NXY + 1, half] for k in range(NXY)]) for half in (left, right))
    store(listeners_ref, listener_features(lx, ly))
    store(senders_ref, sender_features(sx, sy))
    user_ref[0:1, :] = chunk_ref[source, pl.ds(x * 4 + y, 1), :]
    user_ref[1:8, :] = chunk_ref[source, NXY + 1 :, :]


def spread(parts):
    pieces = []
    for k in range(0, 16, 2):
        left = parts[k, BLOCK:, 0:BLOCK]
        right = parts[k + 1, BLOCK:, 0:BLOCK]
        pieces.append(jnp.concatenate([left, right], axis=1))
    features = jnp.concatenate(pieces, axis=1)
    return jnp.concatenate([features, jnp.zeros_like(features)], axis=0).astype(BF16)


def split(value):
    high = value.astype(BF16)
    low = (value - high.astype(F32)).astype(BF16)
    return high, low


def gain_kernel(far, place_ref, plane_ref, column_ref, *rest):
    *before, total_ref = rest
    x, y, z0, z2, z1, zhi, core = (place_ref[i] for i in range(7))
    rows = plane_ref[...]
    columns = spread(column_ref)
    value_high, value_low = split(column_ref[:, 0:BLOCK, :].reshape(HALF, BANDS))
    values = jnp.concatenate([value_high, value_low], axis=1)
    values = jnp.concatenate([values, values], axis=0)
    row_base = zhi * 4096 + core * 2048 + (z2 * 4 + z1 * 2 + z0) * 256
    col_base = y * 8192 + (1 - core if far else core) * 2048 + x * 64
    tile = 128
    for r in range(0, ROWS, tile):
        row = lax.broadcasted_iota(jnp.int32, (tile, tile), 0) + r
        block = row >> 6
        row_id = row_base + (block & 3) * 8192 + (block >> 2) * 64 + (row & 63)
        highs, lows = [], []
        for c in range(0, HALF, tile):
            col = lax.broadcasted_iota(jnp.int32, (1, tile), 1) + c
            zed = col >> 6
            col_id = col_base + (zed >> 3) * 4096 + (zed & 7) * 256 + (col & 63)
            square = lax.dot_general(
                rows[:, r : r + tile],
                columns[:, c : c + tile],
                (((0,), (0,)), ((), ())),
                preferred_element_type=F32,
            )
            guess = pl.reciprocal(square, approx=True)
            gain = guess * (2.0 - square * guess)
            gain = jnp.where(row_id == col_id, 0.0, gain)
            high, low = split(gain)
            highs.append(high)
            lows.append(low)
        gains = jnp.concatenate(highs + lows, axis=1)
        product = jnp.dot(gains, values, preferred_element_type=F32)
        part = product[:, :BANDS] + product[:, BANDS:]
        for ref in before:
            part = part + ref[r : r + tile, :]
        total_ref[r : r + tile, :] = part


def add_blocks(ref):
    total = ref[0]
    for k in range(1, NXY):
        total = total + ref[k]
    return total


def derive_kernel(parts_ref, powers_ref, sent_ref, user_ref, quality_ref, own_ref, column_ref):
    interference = add_blocks(parts_ref)
    lx, ly = user_ref[0:1, 0:BLOCK], user_ref[0:1, BLOCK:]
    dx = lx + 0.5 * sent_ref[BLOCK : BLOCK + 1, 0:BLOCK]
    dy = ly + 0.5 * sent_ref[BLOCK + 1 : BLOCK + 2, 0:BLOCK]
    own_gain = 1.0 / (1.0 + dx * dx + dy * dy)
    weight = WEIGHT_UNIT * user_ref[1:2, 0:BLOCK]
    fair = user_ref[1:2, BLOCK:]
    rows = jnp.concatenate([own_gain, weight, fair, jnp.zeros((5, BLOCK), F32)], axis=0)
    rows = jnp.concatenate([rows, jnp.zeros_like(rows)], axis=1)
    columns = jnp.concatenate([rows, jnp.zeros((120, 128), F32)], axis=0).T
    own_gain = columns[0:BLOCK, 0:1]
    weight = columns[0:BLOCK, 1:2]
    fair = columns[0:BLOCK, 2:3]
    signal = ARRAY_GAIN * own_gain * powers_ref[...]
    denominator = NOISE_POWER + interference
    quality = signal / denominator
    marginal = weight * jnp.exp(-fair * jnp.log(quality)) / denominator
    quality_ref[...] = quality
    own_ref[...] = ARRAY_GAIN * own_gain * marginal
    column_ref[0:BLOCK, :] = marginal * quality
    features = listener_features(lx.astype(jnp.int32), ly.astype(jnp.int32))
    column_ref[BLOCK:, :] = jnp.concatenate([features, jnp.zeros_like(features)], axis=1)


def finish_kernel(place_ref, parts_ref, own_ref, powers_ref, gradient_ref, power_ref, gap_ref):
    gradient = own_ref[...] - add_blocks(parts_ref)
    powers = powers_ref[...]
    target = PEAK_POWER * jax.nn.sigmoid(gradient)
    step_size = place_ref[7].astype(F32) / 4096.0
    gradient_ref[...] = gradient
    power_ref[...] = powers + step_size * (target - powers)
    gap = PEAK_POWER * jnp.maximum(gradient, 0.0) - gradient * powers
    gap = jnp.sum(gap, axis=0, keepdims=True)
    for k in range(2 * NZ):
        gap_ref[k] = gap


def fold_kernel(parts_ref, out_ref):
    total = jnp.sum(parts_ref[...], axis=0)
    for k in range(NXY):
        out_ref[k] = total


def per_device(sender_xy, listener_xy, powers, weight, fairness, step_code):
    place = [lax.axis_index(name).astype(jnp.int32) for name in PLACE]
    place = jnp.stack([*place, step_code[0]])
    to_receiver = [((b % 32) * 16 + b // 32, b) for b in range(512)]
    swap = [(0, 1), (1, 0)]
    block, product = shape(BLOCK, BANDS), shape(ROWS, BANDS)
    work = dict(flops=2 * ROWS * HALF * 512, bytes_accessed=1 << 22)

    def gain_product(far, *args):
        def kernel(*refs):
            gain_kernel(far, *refs)

        return call(kernel, product, 1 + len(args), smem=(0,), **work)(place, *args)

    def spread_sum(near, far, plane):
        part = gain_product(False, plane, near)
        part = gain_product(True, plane, far, part)
        return lax.all_to_all(part.reshape(NXY, BLOCK, BANDS), XY, 0, 0)

    info = jnp.concatenate([sender_xy, listener_xy, weight[None], fairness[None]], axis=0)
    sent = call(pack_kernel, shape(SENT, BANDS), 2)(info, powers)
    near = lax.all_gather(sent, Z, axis=0)
    far = lax.ppermute(near, "core", swap)
    chunks = call(chunk_kernel, shape(NXY, 24, BANDS), 4, smem=(0,))(place, near, far, sent)
    chunks = lax.all_to_all(chunks, XY, 0, 0)
    features = shape(16, ROWS, dtype=BF16)
    listeners, senders, user = call(
        plane_kernel, (features, features, shape(8, BANDS)), 2, smem=(0,)
    )(place, chunks)
    parts = spread_sum(near, far, listeners)
    quality, own, column = call(derive_kernel, (block, block, shape(SENT, BANDS)), 4)(
        parts, powers, sent, user
    )

    near = lax.all_gather(column, Z, axis=0)
    far = lax.ppermute(near, "core", swap)
    parts = spread_sum(near, far, senders)
    gradient, new_power, gap = call(
        finish_kernel, (block, block, shape(2 * NZ, 1, BANDS)), 4, smem=(0,)
    )(place, parts, own, powers)

    quality = lax.ppermute(quality, AXES, to_receiver)
    gap = lax.all_to_all(gap, (*Z, "core"), 0, 0)
    gap = call(fold_kernel, shape(NXY, 1, BANDS), 1)(gap)
    gap = lax.all_to_all(gap, XY, 0, 0)
    return quality, gradient, new_power, (jnp.sum(gap) / (USERS * BANDS)).reshape(1)


def solution(mesh):
    fine = Mesh(mesh.devices.reshape(SIZES), AXES)
    rx, tx = ("z2", "z1", "z0", "x"), ("y", "zhi", "core")
    by_sender, by_receiver = (*tx, *rx), (*rx, *tx)
    return jax.shard_map(
        per_device,
        mesh=fine,
        in_specs=(
            P(None, by_sender),
            P(None, by_receiver),
            P(by_sender, None),
            P(by_receiver),
            P(by_receiver),
            P(),
        ),
        out_specs=(P(by_receiver, None), P(by_sender, None), P(by_sender, None), P()),
        check_vma=False,
    )
```

```python
import jax
import jax.numpy as jnp
from jax import lax
from jax.experimental import pallas as pl
from jax.experimental.pallas import tpu as pltpu
from jax.sharding import Mesh
from jax.sharding import PartitionSpec as P

NOISE_POWER = 0.05
ARRAY_GAIN = 32.0
WEIGHT_UNIT = 1.0 / 16.0
PEAK_POWER = 1.0

AXES = ("z2", "z1", "z0", "x", "y", "zhi", "core")
SIZES = (2, 2, 2, 4, 4, 2, 2)
Z = ("zhi", "z2", "z1", "z0")
XY = ("x", "y")
PLACE = ("x", "y", "z0", "z2", "z1", "zhi", "core")
NZ, NXY = 16, 16
BLOCK, BANDS = 64, 128
SENT = BLOCK + 8
HALF = NZ * BLOCK
ROWS = NXY * BLOCK
USERS = 32768
VMEM_LIMIT = 20 * 1024 * 1024
F32, BF16 = jnp.float32, jnp.bfloat16


def whole():
    return pl.BlockSpec(memory_space=pltpu.VMEM)


def call(kernel, outs, n_in, flops=0, bytes_accessed=1 << 20, smem=()):
    def spec(i):
        return pl.BlockSpec(memory_space=pltpu.SMEM) if i in smem else whole()

    many = isinstance(outs, (list, tuple))
    return pl.pallas_call(
        kernel,
        out_shape=outs,
        in_specs=[spec(i) for i in range(n_in)],
        out_specs=[whole() for _ in outs] if many else whole(),
        compiler_params=pltpu.CompilerParams(vmem_limit_bytes=VMEM_LIMIT),
        cost_estimate=pl.CostEstimate(flops=flops, bytes_accessed=bytes_accessed, transcendentals=0),
    )


def shape(*dims, dtype=F32):
    return jax.ShapeDtypeStruct(dims, dtype)


def split_norm(norm):
    low = norm & 511
    odd = low & 1
    return norm - low, low - odd, odd


def listener_features(lx, ly):
    one = jnp.ones_like(lx)
    l1, l2, l3 = split_norm(lx * lx + ly * ly + 1)
    return jnp.concatenate([lx, ly, l1, l2, l3, one, one, one], axis=0).astype(F32)


def sender_features(sx, sy):
    one = jnp.ones_like(sx)
    s1, s2, s3 = split_norm(sx * sx + sy * sy)
    return jnp.concatenate([-2 * sx, -2 * sy, one, one, one, s1, s2, s3], axis=0).astype(F32)


def pack_kernel(info_ref, powers_ref, sent_ref):
    sent = sender_features(info_ref[0:1, :], info_ref[1:2, :])
    user = jnp.concatenate([info_ref[2:6, :].astype(F32), jnp.zeros((4, BLOCK), F32)], axis=0)
    sent_ref[0:BLOCK, :] = powers_ref[...]
    sent_ref[BLOCK:, :] = jnp.concatenate([sent, user], axis=1)


def chunk_kernel(place_ref, near_ref, far_ref, sent_ref, chunk_ref):
    zhi, core = place_ref[5], place_ref[6]
    users = []
    for k in range(NXY):
        there_x, there_y = k >> 2, k & 3
        at = (there_x >> 1) * 8 + there_y * 2 + zhi
        near, far = near_ref[at, BLOCK:, BLOCK:], far_ref[at, BLOCK:, BLOCK:]
        users.append(jnp.where(core == there_x & 1, near, far))
    places = [jnp.concatenate([user[0:1], user[1:2]], axis=1) for user in users]
    places = jnp.concatenate(places, axis=0)
    sender = -0.5 * sent_ref[BLOCK : BLOCK + 2, 0:BLOCK]
    sender = jnp.concatenate([sender[0:1], sender[1:2]], axis=1)
    for k, user in enumerate(users):
        weights = jnp.concatenate([user[2:3], user[3:4]], axis=1)
        tail = jnp.concatenate([sender, weights, jnp.zeros((6, BANDS), F32)], axis=0)
        chunk_ref[k, 0:NXY, :] = places
        chunk_ref[k, NXY:, :] = tail


def plane_kernel(place_ref, chunk_ref, listeners_ref, senders_ref, user_ref):
    x, y, z0, z2, z1, zhi, core = (place_ref[i] for i in range(7))
    source = (core * 2 + z2) * 4 + z1 * 2 + z0

    def line(pieces):
        pairs = [jnp.concatenate(pieces[k : k + 2], axis=1) for k in range(0, NXY, 2)]
        return jnp.concatenate(pairs, axis=1).astype(jnp.int32)

    def store(ref, features):
        ref[...] = jnp.concatenate([features, jnp.zeros_like(features)], axis=0).astype(BF16)

    left, right = slice(0, BLOCK), slice(BLOCK, 2 * BLOCK)
    places = chunk_ref[source, 0:NXY, :]
    lx, ly = (line([places[k : k + 1, half] for k in range(NXY)]) for half in (left, right))
    sx, sy = (line([chunk_ref[k, NXY : NXY + 1, half] for k in range(NXY)]) for half in (left, right))
    store(listeners_ref, listener_features(lx, ly))
    store(senders_ref, sender_features(sx, sy))
    user_ref[0:1, :] = chunk_ref[source, pl.ds(x * 4 + y, 1), :]
    user_ref[1:8, :] = chunk_ref[source, NXY + 1 :, :]


def spread(parts):
    pieces = []
    for k in range(0, 16, 2):
        left = parts[k, BLOCK:, 0:BLOCK]
        right = parts[k + 1, BLOCK:, 0:BLOCK]
        pieces.append(jnp.concatenate([left, right], axis=1))
    features = jnp.concatenate(pieces, axis=1)
    return jnp.concatenate([features, jnp.zeros_like(features)], axis=0).astype(BF16)


def split(value):
    high = value.astype(BF16)
    low = (value - high.astype(F32)).astype(BF16)
    return high, low


def gain_kernel(far, place_ref, plane_ref, column_ref, *rest):
    *before, total_ref = rest
    x, y, z0, z2, z1, zhi, core = (place_ref[i] for i in range(7))
    rows = plane_ref[...]
    columns = spread(column_ref)
    value_high, value_low = split(column_ref[:, 0:BLOCK, :].reshape(HALF, BANDS))
    values = jnp.concatenate([value_high, value_low], axis=1)
    values = jnp.concatenate([values, values], axis=0)
    row_base = zhi * 4096 + core * 2048 + (z2 * 4 + z1 * 2 + z0) * 256
    col_base = y * 8192 + core * 2048 + x * 64
    tile = 128
    for r in range(0, ROWS, tile):
        row = lax.broadcasted_iota(jnp.int32, (tile, tile), 0) + r
        block = row >> 6
        row_id = row_base + (block & 3) * 8192 + (block >> 2) * 64 + (row & 63)
        highs, lows = [], []
        for c in range(0, HALF, tile):
            col = lax.broadcasted_iota(jnp.int32, (1, tile), 1) + c
            zed = col >> 6
            col_id = col_base + (zed >> 3) * 4096 + (zed & 7) * 256 + (col & 63)
            square = lax.dot_general(
                rows[:, r : r + tile],
                columns[:, c : c + tile],
                (((0,), (0,)), ((), ())),
                preferred_element_type=F32,
            )
            guess = pl.reciprocal(square, approx=True)
            gain = guess * (2.0 - square * guess)
            if not far:
                gain = jnp.where(row_id == col_id, 0.0, gain)
            high, low = split(gain)
            highs.append(high)
            lows.append(low)
        gains = jnp.concatenate(highs + lows, axis=1)
        product = jnp.dot(gains, values, preferred_element_type=F32)
        part = product[:, :BANDS] + product[:, BANDS:]
        for ref in before:
            part = part + ref[r : r + tile, :]
        total_ref[r : r + tile, :] = part


def add_blocks(ref):
    total = ref[0]
    for k in range(1, NXY):
        total = total + ref[k]
    return total


def derive_kernel(parts_ref, powers_ref, sent_ref, user_ref, quality_ref, own_ref, column_ref):
    interference = add_blocks(parts_ref)
    lx, ly = user_ref[0:1, 0:BLOCK], user_ref[0:1, BLOCK:]
    dx = lx + 0.5 * sent_ref[BLOCK : BLOCK + 1, 0:BLOCK]
    dy = ly + 0.5 * sent_ref[BLOCK + 1 : BLOCK + 2, 0:BLOCK]
    own_gain = 1.0 / (1.0 + dx * dx + dy * dy)
    weight = WEIGHT_UNIT * user_ref[1:2, 0:BLOCK]
    fair = user_ref[1:2, BLOCK:]
    rows = jnp.concatenate([own_gain, weight, fair, jnp.zeros((5, BLOCK), F32)], axis=0)
    rows = jnp.concatenate([rows, jnp.zeros_like(rows)], axis=1)
    columns = jnp.concatenate([rows, jnp.zeros((120, 128), F32)], axis=0).T
    own_gain = columns[0:BLOCK, 0:1]
    weight = columns[0:BLOCK, 1:2]
    fair = columns[0:BLOCK, 2:3]
    signal = ARRAY_GAIN * own_gain * powers_ref[...]
    denominator = NOISE_POWER + interference
    quality = signal / denominator
    marginal = weight * jnp.exp(-fair * jnp.log(quality)) / denominator
    quality_ref[...] = quality
    own_ref[...] = ARRAY_GAIN * own_gain * marginal
    column_ref[0:BLOCK, :] = marginal * quality
    features = listener_features(lx.astype(jnp.int32), ly.astype(jnp.int32))
    column_ref[BLOCK:, :] = jnp.concatenate([features, jnp.zeros_like(features)], axis=1)


def finish_kernel(place_ref, parts_ref, own_ref, powers_ref, gradient_ref, power_ref, gap_ref):
    gradient = own_ref[...] - add_blocks(parts_ref)
    powers = powers_ref[...]
    target = PEAK_POWER * jax.nn.sigmoid(gradient)
    step_size = place_ref[7].astype(F32) / 4096.0
    gradient_ref[...] = gradient
    power_ref[...] = powers + step_size * (target - powers)
    gap = PEAK_POWER * jnp.maximum(gradient, 0.0) - gradient * powers
    gap = jnp.sum(gap, axis=0, keepdims=True)
    for k in range(2 * NZ):
        gap_ref[k] = gap


def fold_kernel(parts_ref, out_ref):
    total = jnp.sum(parts_ref[...], axis=0)
    for k in range(NXY):
        out_ref[k] = total


def last_kernel(parts_ref, late_ref, gap_ref, quality_ref):
    total = jnp.sum(jnp.sum(parts_ref[...], axis=0), axis=1, keepdims=True)
    gap_ref[...] = total / (USERS * BANDS)
    quality_ref[...] = late_ref[...]


def per_device(sender_xy, listener_xy, powers, weight, fairness, step_code):
    place = [lax.axis_index(name).astype(jnp.int32) for name in PLACE]
    place = jnp.stack([*place, step_code[0]])
    to_receiver = [((b % 32) * 16 + b // 32, b) for b in range(512)]
    swap = [(0, 1), (1, 0)]
    block, product = shape(BLOCK, BANDS), shape(ROWS, BANDS)
    work = dict(flops=2 * ROWS * HALF * 512, bytes_accessed=1 << 22)

    def gain_product(far, *args):
        def kernel(*refs):
            gain_kernel(far, *refs)

        return call(kernel, product, 1 + len(args), smem=(0,), **work)(place, *args)

    def spread_sum(near, far, plane):
        part = gain_product(False, plane, near)
        part = gain_product(True, plane, far, part)
        return lax.all_to_all(part.reshape(NXY, BLOCK, BANDS), XY, 0, 0)

    info = jnp.concatenate([sender_xy, listener_xy, weight[None], fairness[None]], axis=0)
    sent = call(pack_kernel, shape(SENT, BANDS), 2)(info, powers)
    near = lax.all_gather(sent, Z, axis=0)
    far = lax.ppermute(near, "core", swap)
    chunks = call(chunk_kernel, shape(NXY, 24, BANDS), 4, smem=(0,))(place, near, far, sent)
    chunks = lax.all_to_all(chunks, XY, 0, 0)
    features = shape(16, ROWS, dtype=BF16)
    listeners, senders, user = call(
        plane_kernel, (features, features, shape(8, BANDS)), 2, smem=(0,)
    )(place, chunks)
    parts = spread_sum(near, far, listeners)
    quality, own, column = call(derive_kernel, (block, block, shape(SENT, BANDS)), 4)(
        parts, powers, sent, user
    )

    near = lax.all_gather(column, Z, axis=0)
    far = lax.ppermute(near, "core", swap)
    parts = spread_sum(near, far, senders)
    gradient, new_power, gap = call(
        finish_kernel, (block, block, shape(2 * NZ, 1, BANDS)), 4, smem=(0,)
    )(place, parts, own, powers)

    quality = lax.ppermute(quality, AXES, to_receiver)
    gap = lax.all_to_all(gap, (*Z, "core"), 0, 0)
    gap = call(fold_kernel, shape(NXY, 1, BANDS), 1)(gap)
    gap = lax.all_to_all(gap, XY, 0, 0)
    gap, quality = call(last_kernel, (shape(1, 1), block), 2)(gap, quality)
    return quality, gradient, new_power, gap.reshape(1)


def solution(mesh):
    fine = Mesh(mesh.devices.reshape(SIZES), AXES)
    rx, tx = ("z2", "z1", "z0", "x"), ("y", "zhi", "core")
    by_sender, by_receiver = (*tx, *rx), (*rx, *tx)
    return jax.shard_map(
        per_device,
        mesh=fine,
        in_specs=(
            P(None, by_sender),
            P(None, by_receiver),
            P(by_sender, None),
            P(by_receiver),
            P(by_receiver),
            P(),
        ),
        out_specs=(P(by_receiver, None), P(by_sender, None), P(by_sender, None), P()),
        check_vma=False,
    )
```

```python
import jax
import jax.numpy as jnp
from jax import lax
from jax.experimental import pallas as pl
from jax.experimental.pallas import tpu as pltpu
from jax.sharding import Mesh
from jax.sharding import PartitionSpec as P

NOISE_POWER = 0.05
ARRAY_GAIN = 32.0
WEIGHT_UNIT = 1.0 / 16.0
PEAK_POWER = 1.0

AXES = ("z2", "z1", "z0", "x", "y", "zhi", "core")
SIZES = (2, 2, 2, 4, 4, 2, 2)
Z = ("zhi", "z2", "z1", "z0")
XY = ("x", "y")
PLACE = ("x", "y", "z0", "z2", "z1", "zhi", "core")
NZ, NXY = 16, 16
BLOCK, BANDS = 64, 128
SENT = BLOCK + 8
HALF = NZ * BLOCK
ROWS = NXY * BLOCK
USERS = 32768
VMEM_LIMIT = 20 * 1024 * 1024
F32, BF16 = jnp.float32, jnp.bfloat16


def whole():
    return pl.BlockSpec(memory_space=pltpu.VMEM)


def call(kernel, outs, n_in, flops=0, bytes_accessed=1 << 20, smem=()):
    def spec(i):
        return pl.BlockSpec(memory_space=pltpu.SMEM) if i in smem else whole()

    many = isinstance(outs, (list, tuple))
    return pl.pallas_call(
        kernel,
        out_shape=outs,
        in_specs=[spec(i) for i in range(n_in)],
        out_specs=[whole() for _ in outs] if many else whole(),
        compiler_params=pltpu.CompilerParams(vmem_limit_bytes=VMEM_LIMIT),
        cost_estimate=pl.CostEstimate(flops=flops, bytes_accessed=bytes_accessed, transcendentals=0),
    )


def shape(*dims, dtype=F32):
    return jax.ShapeDtypeStruct(dims, dtype)


def split_norm(norm):
    low = norm & 511
    odd = low & 1
    return norm - low, low - odd, odd


def listener_features(lx, ly):
    one = jnp.ones_like(lx)
    l1, l2, l3 = split_norm(lx * lx + ly * ly + 1)
    return jnp.concatenate([lx, ly, l1, l2, l3, one, one, one], axis=0).astype(F32)


def sender_features(sx, sy):
    one = jnp.ones_like(sx)
    s1, s2, s3 = split_norm(sx * sx + sy * sy)
    return jnp.concatenate([-2 * sx, -2 * sy, one, one, one, s1, s2, s3], axis=0).astype(F32)


def pack_kernel(info_ref, powers_ref, sent_ref):
    sent = sender_features(info_ref[0:1, :], info_ref[1:2, :])
    user = jnp.concatenate([info_ref[2:6, :].astype(F32), jnp.zeros((4, BLOCK), F32)], axis=0)
    sent_ref[0:BLOCK, :] = powers_ref[...]
    sent_ref[BLOCK:, :] = jnp.concatenate([sent, user], axis=1)


def chunk_kernel(place_ref, near_ref, far_ref, sent_ref, chunk_ref):
    zhi, core = place_ref[5], place_ref[6]
    users = []
    for k in range(NXY):
        there_x, there_y = k >> 2, k & 3
        at = (there_x >> 1) * 8 + there_y * 2 + zhi
        near, far = near_ref[at, BLOCK:, BLOCK:], far_ref[at, BLOCK:, BLOCK:]
        users.append(jnp.where(core == there_x & 1, near, far))
    places = [jnp.concatenate([user[0:1], user[1:2]], axis=1) for user in users]
    places = jnp.concatenate(places, axis=0)
    sender = -0.5 * sent_ref[BLOCK : BLOCK + 2, 0:BLOCK]
    sender = jnp.concatenate([sender[0:1], sender[1:2]], axis=1)
    for k, user in enumerate(users):
        weights = jnp.concatenate([user[2:3], user[3:4]], axis=1)
        tail = jnp.concatenate([sender, weights, jnp.zeros((6, BANDS), F32)], axis=0)
        chunk_ref[k, 0:NXY, :] = places
        chunk_ref[k, NXY:, :] = tail


def plane_kernel(place_ref, chunk_ref, listeners_ref, senders_ref, user_ref):
    x, y, z0, z2, z1, zhi, core = (place_ref[i] for i in range(7))
    source = (core * 2 + z2) * 4 + z1 * 2 + z0

    def line(pieces):
        pairs = [jnp.concatenate(pieces[k : k + 2], axis=1) for k in range(0, NXY, 2)]
        return jnp.concatenate(pairs, axis=1).astype(jnp.int32)

    def store(ref, features):
        ref[...] = jnp.concatenate([features, jnp.zeros_like(features)], axis=0).astype(BF16)

    left, right = slice(0, BLOCK), slice(BLOCK, 2 * BLOCK)
    places = chunk_ref[source, 0:NXY, :]
    lx, ly = (line([places[k : k + 1, half] for k in range(NXY)]) for half in (left, right))
    sx, sy = (line([chunk_ref[k, NXY : NXY + 1, half] for k in range(NXY)]) for half in (left, right))
    store(listeners_ref, listener_features(lx, ly))
    store(senders_ref, sender_features(sx, sy))
    user_ref[0:1, :] = chunk_ref[source, pl.ds(x * 4 + y, 1), :]
    user_ref[1:8, :] = chunk_ref[source, NXY + 1 :, :]


def spread(parts):
    pieces = []
    for k in range(0, 16, 2):
        left = parts[k, BLOCK:, 0:BLOCK]
        right = parts[k + 1, BLOCK:, 0:BLOCK]
        pieces.append(jnp.concatenate([left, right], axis=1))
    features = jnp.concatenate(pieces, axis=1)
    return jnp.concatenate([features, jnp.zeros_like(features)], axis=0).astype(BF16)


def split(value):
    high = value.astype(BF16)
    low = (value - high.astype(F32)).astype(BF16)
    return high, low


def gain_kernel(far, place_ref, plane_ref, column_ref, *rest):
    *before, total_ref = rest
    x, y, z0, z2, z1, zhi, core = (place_ref[i] for i in range(7))
    rows = plane_ref[...]
    columns = spread(column_ref)
    value_high, value_low = split(column_ref[:, 0:BLOCK, :].reshape(HALF, BANDS))
    values = jnp.concatenate([value_high, value_low], axis=1)
    values = jnp.concatenate([values, values], axis=0)
    row_base = zhi * 4096 + core * 2048 + (z2 * 4 + z1 * 2 + z0) * 256
    col_base = y * 8192 + core * 2048 + x * 64
    tile = 128
    for r in range(0, ROWS, tile):
        row = lax.broadcasted_iota(jnp.int32, (tile, tile), 0) + r
        block = row >> 6
        row_id = row_base + (block & 3) * 8192 + (block >> 2) * 64 + (row & 63)
        highs, lows = [], []
        for c in range(0, HALF, tile):
            col = lax.broadcasted_iota(jnp.int32, (1, tile), 1) + c
            zed = col >> 6
            col_id = col_base + (zed >> 3) * 4096 + (zed & 7) * 256 + (col & 63)
            square = lax.dot_general(
                rows[:, r : r + tile],
                columns[:, c : c + tile],
                (((0,), (0,)), ((), ())),
                preferred_element_type=F32,
            )
            guess = pl.reciprocal(square, approx=True)
            gain = guess * (2.0 - square * guess)
            if not far:
                gain = jnp.where(row_id == col_id, 0.0, gain)
            high, low = split(gain)
            highs.append(high)
            lows.append(low)
        gains = jnp.concatenate(highs + lows, axis=1)
        product = jnp.dot(gains, values, preferred_element_type=F32)
        part = product[:, :BANDS] + product[:, BANDS:]
        for ref in before:
            part = part + ref[r : r + tile, :]
        total_ref[r : r + tile, :] = part


def add_blocks(ref):
    total = ref[0]
    for k in range(1, NXY):
        total = total + ref[k]
    return total


def derive_kernel(parts_ref, powers_ref, sent_ref, user_ref, quality_ref, own_ref, column_ref):
    interference = add_blocks(parts_ref)
    lx, ly = user_ref[0:1, 0:BLOCK], user_ref[0:1, BLOCK:]
    dx = lx + 0.5 * sent_ref[BLOCK : BLOCK + 1, 0:BLOCK]
    dy = ly + 0.5 * sent_ref[BLOCK + 1 : BLOCK + 2, 0:BLOCK]
    own_gain = 1.0 / (1.0 + dx * dx + dy * dy)
    weight = WEIGHT_UNIT * user_ref[1:2, 0:BLOCK]
    fair = user_ref[1:2, BLOCK:]
    rows = jnp.concatenate([own_gain, weight, fair, jnp.zeros((5, BLOCK), F32)], axis=0)
    rows = jnp.concatenate([rows, jnp.zeros_like(rows)], axis=1)
    columns = jnp.concatenate([rows, jnp.zeros((120, 128), F32)], axis=0).T
    own_gain = columns[0:BLOCK, 0:1]
    weight = columns[0:BLOCK, 1:2]
    fair = columns[0:BLOCK, 2:3]
    signal = ARRAY_GAIN * own_gain * powers_ref[...]
    denominator = NOISE_POWER + interference
    quality = signal / denominator
    marginal = weight * jnp.exp(-fair * jnp.log(quality)) / denominator
    quality_ref[...] = quality
    own_ref[...] = ARRAY_GAIN * own_gain * marginal
    column_ref[0:BLOCK, :] = marginal * quality
    features = listener_features(lx.astype(jnp.int32), ly.astype(jnp.int32))
    column_ref[BLOCK:, :] = jnp.concatenate([features, jnp.zeros_like(features)], axis=1)


def finish_kernel(place_ref, parts_ref, own_ref, powers_ref, gradient_ref, power_ref, gap_ref):
    gradient = own_ref[...] - add_blocks(parts_ref)
    powers = powers_ref[...]
    target = PEAK_POWER * jax.nn.sigmoid(gradient)
    step_size = place_ref[7].astype(F32) / 4096.0
    gradient_ref[...] = gradient
    power_ref[...] = powers + step_size * (target - powers)
    gap = PEAK_POWER * jnp.maximum(gradient, 0.0) - gradient * powers
    gap = jnp.sum(gap, axis=0, keepdims=True)
    for k in range(2 * NZ):
        gap_ref[k] = gap


def fold_kernel(parts_ref, out_ref):
    total = jnp.sum(parts_ref[...], axis=0)
    for k in range(NXY):
        out_ref[k] = total


def last_kernel(parts_ref, late_ref, gap_ref, quality_ref):
    total = jnp.sum(jnp.sum(parts_ref[...], axis=0), axis=1, keepdims=True)
    gap_ref[...] = total / (USERS * BANDS)
    quality_ref[...] = late_ref[...]


def per_device(sender_xy, listener_xy, powers, weight, fairness, step_code):
    place = [lax.axis_index(name).astype(jnp.int32) for name in PLACE]
    place = jnp.stack([*place, step_code[0]])
    to_receiver = [((b % 32) * 16 + b // 32, b) for b in range(512)]
    swap = [(0, 1), (1, 0)]
    block, product = shape(BLOCK, BANDS), shape(ROWS, BANDS)
    work = dict(flops=2 * ROWS * HALF * 512, bytes_accessed=1 << 22)

    def gain_product(far, *args):
        def kernel(*refs):
            gain_kernel(far, *refs)

        return call(kernel, product, 1 + len(args), smem=(0,), **work)(place, *args)

    def spread_sum(near, far, plane):
        part = gain_product(False, plane, near)
        part = gain_product(True, plane, far, part)
        return lax.all_to_all(part.reshape(NXY, BLOCK, BANDS), XY, 0, 0)

    info = jnp.concatenate([sender_xy, listener_xy, weight[None], fairness[None]], axis=0)
    sent = call(pack_kernel, shape(SENT, BANDS), 2)(info, powers)
    near = lax.all_gather(sent, Z, axis=0)
    far = lax.ppermute(near, "core", swap)
    chunks = call(chunk_kernel, shape(NXY, 24, BANDS), 4, smem=(0,))(place, near, far, sent)
    chunks = lax.all_to_all(chunks, XY, 0, 0)
    features = shape(16, ROWS, dtype=BF16)
    listeners, senders, user = call(
        plane_kernel, (features, features, shape(8, BANDS)), 2, smem=(0,)
    )(place, chunks)
    parts = spread_sum(near, far, listeners)
    quality, own, column = call(derive_kernel, (block, block, shape(SENT, BANDS)), 4)(
        parts, powers, sent, user
    )

    near = lax.all_gather(column, Z, axis=0)
    far = lax.ppermute(near, "core", swap)
    parts = spread_sum(near, far, senders)
    gradient, new_power, gap = call(
        finish_kernel, (block, block, shape(2 * NZ, 1, BANDS)), 4, smem=(0,)
    )(place, parts, own, powers)

    quality = lax.ppermute(quality, AXES, to_receiver)
    gap, quality = lax.optimization_barrier((gap, quality))
    gap = lax.all_to_all(gap, (*Z, "core"), 0, 0)
    gap = call(fold_kernel, shape(NXY, 1, BANDS), 1)(gap)
    gap = lax.all_to_all(gap, XY, 0, 0)
    gap, quality = call(last_kernel, (shape(1, 1), block), 2)(gap, quality)
    return quality, gradient, new_power, gap.reshape(1)


def solution(mesh):
    fine = Mesh(mesh.devices.reshape(SIZES), AXES)
    rx, tx = ("z2", "z1", "z0", "x"), ("y", "zhi", "core")
    by_sender, by_receiver = (*tx, *rx), (*rx, *tx)
    return jax.shard_map(
        per_device,
        mesh=fine,
        in_specs=(
            P(None, by_sender),
            P(None, by_receiver),
            P(by_sender, None),
            P(by_receiver),
            P(by_receiver),
            P(),
        ),
        out_specs=(P(by_receiver, None), P(by_sender, None), P(by_sender, None), P()),
        check_vma=False,
    )
```

```python
import jax
import jax.numpy as jnp
from jax import lax
from jax.experimental import pallas as pl
from jax.experimental.pallas import tpu as pltpu
from jax.sharding import Mesh
from jax.sharding import PartitionSpec as P

NOISE_POWER = 0.05
ARRAY_GAIN = 32.0
WEIGHT_UNIT = 1.0 / 16.0
PEAK_POWER = 1.0

AXES = ("z2", "z1", "z0", "x", "y", "zhi", "core")
SIZES = (2, 2, 2, 4, 4, 2, 2)
Z = ("zhi", "z2", "z1", "z0")
XY = ("x", "y")
PLACE = ("x", "y", "z0", "z2", "z1", "zhi", "core")
NZ, NXY = 16, 16
BLOCK, BANDS = 64, 128
SENT = BLOCK + 8
HALF = NZ * BLOCK
ROWS = NXY * BLOCK
USERS = 32768
VMEM_LIMIT = 20 * 1024 * 1024
F32, BF16 = jnp.float32, jnp.bfloat16


def whole():
    return pl.BlockSpec(memory_space=pltpu.VMEM)


def call(kernel, outs, n_in, flops=0, bytes_accessed=1 << 20, smem=()):
    def spec(i):
        return pl.BlockSpec(memory_space=pltpu.SMEM) if i in smem else whole()

    many = isinstance(outs, (list, tuple))
    return pl.pallas_call(
        kernel,
        out_shape=outs,
        in_specs=[spec(i) for i in range(n_in)],
        out_specs=[whole() for _ in outs] if many else whole(),
        compiler_params=pltpu.CompilerParams(vmem_limit_bytes=VMEM_LIMIT),
        cost_estimate=pl.CostEstimate(flops=flops, bytes_accessed=bytes_accessed, transcendentals=0),
    )


def shape(*dims, dtype=F32):
    return jax.ShapeDtypeStruct(dims, dtype)


def split_norm(norm):
    low = norm & 511
    odd = low & 1
    return norm - low, low - odd, odd


def listener_features(lx, ly):
    one = jnp.ones_like(lx)
    l1, l2, l3 = split_norm(lx * lx + ly * ly + 1)
    return jnp.concatenate([lx, ly, l1, l2, l3, one, one, one], axis=0).astype(F32)


def sender_features(sx, sy):
    one = jnp.ones_like(sx)
    s1, s2, s3 = split_norm(sx * sx + sy * sy)
    return jnp.concatenate([-2 * sx, -2 * sy, one, one, one, s1, s2, s3], axis=0).astype(F32)


def pack_kernel(info_ref, powers_ref, sent_ref):
    sent = sender_features(info_ref[0:1, :], info_ref[1:2, :])
    user = jnp.concatenate([info_ref[2:6, :].astype(F32), jnp.zeros((4, BLOCK), F32)], axis=0)
    sent_ref[0:BLOCK, :] = powers_ref[...]
    sent_ref[BLOCK:, :] = jnp.concatenate([sent, user], axis=1)


def chunk_kernel(place_ref, near_ref, far_ref, sent_ref, chunk_ref):
    zhi, core = place_ref[5], place_ref[6]
    users = []
    for k in range(NXY):
        there_x, there_y = k >> 2, k & 3
        at = (there_x >> 1) * 8 + there_y * 2 + zhi
        near, far = near_ref[at, BLOCK:, BLOCK:], far_ref[at, BLOCK:, BLOCK:]
        users.append(jnp.where(core == there_x & 1, near, far))
    places = [jnp.concatenate([user[0:1], user[1:2]], axis=1) for user in users]
    places = jnp.concatenate(places, axis=0)
    sender = -0.5 * sent_ref[BLOCK : BLOCK + 2, 0:BLOCK]
    sender = jnp.concatenate([sender[0:1], sender[1:2]], axis=1)
    for k, user in enumerate(users):
        weights = jnp.concatenate([user[2:3], user[3:4]], axis=1)
        tail = jnp.concatenate([sender, weights, jnp.zeros((6, BANDS), F32)], axis=0)
        chunk_ref[k, 0:NXY, :] = places
        chunk_ref[k, NXY:, :] = tail


def plane_kernel(place_ref, chunk_ref, listeners_ref, senders_ref, user_ref):
    x, y, z0, z2, z1, zhi, core = (place_ref[i] for i in range(7))
    source = (core * 2 + z2) * 4 + z1 * 2 + z0

    def line(pieces):
        pairs = [jnp.concatenate(pieces[k : k + 2], axis=1) for k in range(0, NXY, 2)]
        return jnp.concatenate(pairs, axis=1).astype(jnp.int32)

    def store(ref, features):
        ref[...] = jnp.concatenate([features, jnp.zeros_like(features)], axis=0).astype(BF16)

    left, right = slice(0, BLOCK), slice(BLOCK, 2 * BLOCK)
    places = chunk_ref[source, 0:NXY, :]
    lx, ly = (line([places[k : k + 1, half] for k in range(NXY)]) for half in (left, right))
    sx, sy = (line([chunk_ref[k, NXY : NXY + 1, half] for k in range(NXY)]) for half in (left, right))
    store(listeners_ref, listener_features(lx, ly))
    store(senders_ref, sender_features(sx, sy))
    user_ref[0:1, :] = chunk_ref[source, pl.ds(x * 4 + y, 1), :]
    user_ref[1:8, :] = chunk_ref[source, NXY + 1 :, :]


def spread(parts):
    pieces = []
    for k in range(0, 16, 2):
        left = parts[k, BLOCK:, 0:BLOCK]
        right = parts[k + 1, BLOCK:, 0:BLOCK]
        pieces.append(jnp.concatenate([left, right], axis=1))
    features = jnp.concatenate(pieces, axis=1)
    return jnp.concatenate([features, jnp.zeros_like(features)], axis=0).astype(BF16)


def split(value):
    high = value.astype(BF16)
    low = (value - high.astype(F32)).astype(BF16)
    return high, low


def gain_kernel(far, place_ref, plane_ref, column_ref, *rest):
    *before, total_ref = rest
    x, y, z0, z2, z1, zhi, core = (place_ref[i] for i in range(7))
    rows = plane_ref[...]
    columns = spread(column_ref)
    value_high, value_low = split(column_ref[:, 0:BLOCK, :].reshape(HALF, BANDS))
    values = jnp.concatenate([value_high, value_low], axis=1)
    values = jnp.concatenate([values, values], axis=0)
    row_base = zhi * 4096 + core * 2048 + (z2 * 4 + z1 * 2 + z0) * 256
    col_base = y * 8192 + core * 2048 + x * 64
    tile = 128
    for r in range(0, ROWS, tile):
        row = lax.broadcasted_iota(jnp.int32, (tile, tile), 0) + r
        block = row >> 6
        row_id = row_base + (block & 3) * 8192 + (block >> 2) * 64 + (row & 63)
        highs, lows = [], []
        for c in range(0, HALF, tile):
            col = lax.broadcasted_iota(jnp.int32, (1, tile), 1) + c
            zed = col >> 6
            col_id = col_base + (zed >> 3) * 4096 + (zed & 7) * 256 + (col & 63)
            square = lax.dot_general(
                rows[:, r : r + tile],
                columns[:, c : c + tile],
                (((0,), (0,)), ((), ())),
                preferred_element_type=F32,
            )
            guess = pl.reciprocal(square, approx=True)
            gain = guess * (2.0 - square * guess)
            if not far:
                gain = jnp.where(row_id == col_id, 0.0, gain)
            high, low = split(gain)
            highs.append(high)
            lows.append(low)
        gains = jnp.concatenate(highs + lows, axis=1)
        product = jnp.dot(gains, values, preferred_element_type=F32)
        part = product[:, :BANDS] + product[:, BANDS:]
        for ref in before:
            part = part + ref[r : r + tile, :]
        total_ref[r : r + tile, :] = part


def add_blocks(ref):
    total = ref[0]
    for k in range(1, NXY):
        total = total + ref[k]
    return total


def derive_kernel(parts_ref, powers_ref, sent_ref, user_ref, quality_ref, own_ref, column_ref):
    interference = add_blocks(parts_ref)
    lx, ly = user_ref[0:1, 0:BLOCK], user_ref[0:1, BLOCK:]
    dx = lx + 0.5 * sent_ref[BLOCK : BLOCK + 1, 0:BLOCK]
    dy = ly + 0.5 * sent_ref[BLOCK + 1 : BLOCK + 2, 0:BLOCK]
    own_gain = 1.0 / (1.0 + dx * dx + dy * dy)
    weight = WEIGHT_UNIT * user_ref[1:2, 0:BLOCK]
    fair = user_ref[1:2, BLOCK:]
    rows = jnp.concatenate([own_gain, weight, fair, jnp.zeros((5, BLOCK), F32)], axis=0)
    rows = jnp.concatenate([rows, jnp.zeros_like(rows)], axis=1)
    columns = jnp.concatenate([rows, jnp.zeros((120, 128), F32)], axis=0).T
    own_gain = columns[0:BLOCK, 0:1]
    weight = columns[0:BLOCK, 1:2]
    fair = columns[0:BLOCK, 2:3]
    signal = ARRAY_GAIN * own_gain * powers_ref[...]
    denominator = NOISE_POWER + interference
    quality = signal / denominator
    marginal = weight * jnp.exp(-fair * jnp.log(quality)) / denominator
    quality_ref[...] = quality
    own_ref[...] = ARRAY_GAIN * own_gain * marginal
    column_ref[0:BLOCK, :] = marginal * quality
    features = listener_features(lx.astype(jnp.int32), ly.astype(jnp.int32))
    column_ref[BLOCK:, :] = jnp.concatenate([features, jnp.zeros_like(features)], axis=1)


def finish_kernel(place_ref, parts_ref, own_ref, powers_ref, gradient_ref, power_ref, gap_ref):
    gradient = own_ref[...] - add_blocks(parts_ref)
    powers = powers_ref[...]
    target = PEAK_POWER * jax.nn.sigmoid(gradient)
    step_size = place_ref[7].astype(F32) / 4096.0
    gradient_ref[...] = gradient
    power_ref[...] = powers + step_size * (target - powers)
    gap = PEAK_POWER * jnp.maximum(gradient, 0.0) - gradient * powers
    gap = jnp.sum(gap, axis=0, keepdims=True)
    for k in range(2 * NXY):
        gap_ref[k] = gap


def fold_kernel(parts_ref, out_ref):
    total = jnp.sum(parts_ref[...], axis=0)
    for k in range(NZ):
        out_ref[k] = total


def last_kernel(parts_ref, late_ref, gap_ref, quality_ref):
    total = jnp.sum(jnp.sum(parts_ref[...], axis=0), axis=1, keepdims=True)
    gap_ref[...] = total / (USERS * BANDS)
    quality_ref[...] = late_ref[...]


def per_device(sender_xy, listener_xy, powers, weight, fairness, step_code):
    place = [lax.axis_index(name).astype(jnp.int32) for name in PLACE]
    place = jnp.stack([*place, step_code[0]])
    to_receiver = [((b % 32) * 16 + b // 32, b) for b in range(512)]
    swap = [(0, 1), (1, 0)]
    block, product = shape(BLOCK, BANDS), shape(ROWS, BANDS)
    work = dict(flops=2 * ROWS * HALF * 512, bytes_accessed=1 << 22)

    def gain_product(far, *args):
        def kernel(*refs):
            gain_kernel(far, *refs)

        return call(kernel, product, 1 + len(args), smem=(0,), **work)(place, *args)

    def spread_sum(near, far, plane):
        part = gain_product(False, plane, near)
        part = gain_product(True, plane, far, part)
        return lax.all_to_all(part.reshape(NXY, BLOCK, BANDS), XY, 0, 0)

    info = jnp.concatenate([sender_xy, listener_xy, weight[None], fairness[None]], axis=0)
    sent = call(pack_kernel, shape(SENT, BANDS), 2)(info, powers)
    near = lax.all_gather(sent, Z, axis=0)
    far = lax.ppermute(near, "core", swap)
    chunks = call(chunk_kernel, shape(NXY, 24, BANDS), 4, smem=(0,))(place, near, far, sent)
    chunks = lax.all_to_all(chunks, XY, 0, 0)
    features = shape(16, ROWS, dtype=BF16)
    listeners, senders, user = call(
        plane_kernel, (features, features, shape(8, BANDS)), 2, smem=(0,)
    )(place, chunks)
    parts = spread_sum(near, far, listeners)
    quality, own, column = call(derive_kernel, (block, block, shape(SENT, BANDS)), 4)(
        parts, powers, sent, user
    )

    near = lax.all_gather(column, Z, axis=0)
    far = lax.ppermute(near, "core", swap)
    parts = spread_sum(near, far, senders)
    gradient, new_power, gap = call(
        finish_kernel, (block, block, shape(2 * NXY, 1, BANDS)), 4, smem=(0,)
    )(place, parts, own, powers)

    quality = lax.ppermute(quality, AXES, to_receiver)
    gap = lax.all_to_all(gap, (*XY, "core"), 0, 0)
    gap = call(fold_kernel, shape(NZ, 1, BANDS), 1)(gap)
    gap = lax.all_to_all(gap, Z, 0, 0)
    gap, quality = call(last_kernel, (shape(1, 1), block), 2)(gap, quality)
    return quality, gradient, new_power, gap.reshape(1)


def solution(mesh):
    fine = Mesh(mesh.devices.reshape(SIZES), AXES)
    rx, tx = ("z2", "z1", "z0", "x"), ("y", "zhi", "core")
    by_sender, by_receiver = (*tx, *rx), (*rx, *tx)
    return jax.shard_map(
        per_device,
        mesh=fine,
        in_specs=(
            P(None, by_sender),
            P(None, by_receiver),
            P(by_sender, None),
            P(by_receiver),
            P(by_receiver),
            P(),
        ),
        out_specs=(P(by_receiver, None), P(by_sender, None), P(by_sender, None), P()),
        check_vma=False,
    )
```

```python
import jax
import jax.numpy as jnp
from jax import lax
from jax.experimental import pallas as pl
from jax.experimental.pallas import tpu as pltpu
from jax.sharding import Mesh
from jax.sharding import PartitionSpec as P

NOISE_POWER = 0.05
ARRAY_GAIN = 32.0
WEIGHT_UNIT = 1.0 / 16.0
PEAK_POWER = 1.0

AXES = ("z2", "z1", "z0", "x", "y", "zhi", "core")
SIZES = (2, 2, 2, 4, 4, 2, 2)
Z = ("zhi", "z2", "z1", "z0")
XY = ("x", "y")
PLACE = ("x", "y", "z0", "z2", "z1", "zhi", "core")
NZ, NXY = 16, 16
BLOCK, BANDS = 64, 128
SENT = BLOCK + 8
HALF = NZ * BLOCK
ROWS = NXY * BLOCK
USERS = 32768
VMEM_LIMIT = 20 * 1024 * 1024
F32, BF16 = jnp.float32, jnp.bfloat16


def whole():
    return pl.BlockSpec(memory_space=pltpu.VMEM)


def call(kernel, outs, n_in, flops=0, bytes_accessed=1 << 20, smem=()):
    def spec(i):
        return pl.BlockSpec(memory_space=pltpu.SMEM) if i in smem else whole()

    many = isinstance(outs, (list, tuple))
    return pl.pallas_call(
        kernel,
        out_shape=outs,
        in_specs=[spec(i) for i in range(n_in)],
        out_specs=[whole() for _ in outs] if many else whole(),
        compiler_params=pltpu.CompilerParams(vmem_limit_bytes=VMEM_LIMIT),
        cost_estimate=pl.CostEstimate(flops=flops, bytes_accessed=bytes_accessed, transcendentals=0),
    )


def shape(*dims, dtype=F32):
    return jax.ShapeDtypeStruct(dims, dtype)


def split_norm(norm):
    low = norm & 511
    odd = low & 1
    return norm - low, low - odd, odd


def listener_features(lx, ly):
    one = jnp.ones_like(lx)
    l1, l2, l3 = split_norm(lx * lx + ly * ly + 1)
    return jnp.concatenate([lx, ly, l1, l2, l3, one, one, one], axis=0).astype(F32)


def sender_features(sx, sy):
    one = jnp.ones_like(sx)
    s1, s2, s3 = split_norm(sx * sx + sy * sy)
    return jnp.concatenate([-2 * sx, -2 * sy, one, one, one, s1, s2, s3], axis=0).astype(F32)


def pack_kernel(info_ref, powers_ref, sent_ref):
    sent = sender_features(info_ref[0:1, :], info_ref[1:2, :])
    user = jnp.concatenate([info_ref[2:6, :].astype(F32), jnp.zeros((4, BLOCK), F32)], axis=0)
    sent_ref[0:BLOCK, :] = powers_ref[...]
    sent_ref[BLOCK:, :] = jnp.concatenate([sent, user], axis=1)


def chunk_kernel(place_ref, near_ref, far_ref, sent_ref, chunk_ref):
    zhi, core = place_ref[5], place_ref[6]
    users = []
    for k in range(NXY):
        there_x, there_y = k >> 2, k & 3
        at = (there_x >> 1) * 8 + there_y * 2 + zhi
        near, far = near_ref[at, BLOCK:, BLOCK:], far_ref[at, BLOCK:, BLOCK:]
        users.append(jnp.where(core == there_x & 1, near, far))
    places = [jnp.concatenate([user[0:1], user[1:2]], axis=1) for user in users]
    places = jnp.concatenate(places, axis=0)
    sender = -0.5 * sent_ref[BLOCK : BLOCK + 2, 0:BLOCK]
    sender = jnp.concatenate([sender[0:1], sender[1:2]], axis=1)
    for k, user in enumerate(users):
        weights = jnp.concatenate([user[2:3], user[3:4]], axis=1)
        tail = jnp.concatenate([sender, weights, jnp.zeros((6, BANDS), F32)], axis=0)
        chunk_ref[k, 0:NXY, :] = places
        chunk_ref[k, NXY:, :] = tail


def plane_kernel(place_ref, chunk_ref, listeners_ref, senders_ref, user_ref):
    x, y, z0, z2, z1, zhi, core = (place_ref[i] for i in range(7))
    source = (core * 2 + z2) * 4 + z1 * 2 + z0

    def line(pieces):
        pairs = [jnp.concatenate(pieces[k : k + 2], axis=1) for k in range(0, NXY, 2)]
        return jnp.concatenate(pairs, axis=1).astype(jnp.int32)

    def store(ref, features):
        ref[...] = jnp.concatenate([features, jnp.zeros_like(features)], axis=0).astype(BF16)

    left, right = slice(0, BLOCK), slice(BLOCK, 2 * BLOCK)
    places = chunk_ref[source, 0:NXY, :]
    lx, ly = (line([places[k : k + 1, half] for k in range(NXY)]) for half in (left, right))
    sx, sy = (line([chunk_ref[k, NXY : NXY + 1, half] for k in range(NXY)]) for half in (left, right))
    store(listeners_ref, listener_features(lx, ly))
    store(senders_ref, sender_features(sx, sy))
    user_ref[0:1, :] = chunk_ref[source, pl.ds(x * 4 + y, 1), :]
    user_ref[1:8, :] = chunk_ref[source, NXY + 1 :, :]


def spread(parts):
    pieces = []
    for k in range(0, 16, 2):
        left = parts[k, BLOCK:, 0:BLOCK]
        right = parts[k + 1, BLOCK:, 0:BLOCK]
        pieces.append(jnp.concatenate([left, right], axis=1))
    features = jnp.concatenate(pieces, axis=1)
    return jnp.concatenate([features, jnp.zeros_like(features)], axis=0).astype(BF16)


def split(value):
    high = value.astype(BF16)
    low = (value - high.astype(F32)).astype(BF16)
    return high, low


def gain_kernel(far, place_ref, plane_ref, column_ref, *rest):
    *before, total_ref = rest
    x, y, z0, z2, z1, zhi, core = (place_ref[i] for i in range(7))
    rows = plane_ref[...]
    columns = spread(column_ref)
    value_high, value_low = split(column_ref[:, 0:BLOCK, :].reshape(HALF, BANDS))
    values = jnp.concatenate([value_high, value_low], axis=1)
    values = jnp.concatenate([values, values], axis=0)
    row_base = zhi * 4096 + core * 2048 + (z2 * 4 + z1 * 2 + z0) * 256
    col_base = y * 8192 + core * 2048 + x * 64
    tile = 128
    for r in range(0, ROWS, tile):
        row = lax.broadcasted_iota(jnp.int32, (tile, tile), 0) + r
        block = row >> 6
        row_id = row_base + (block & 3) * 8192 + (block >> 2) * 64 + (row & 63)
        highs, lows = [], []
        for c in range(0, HALF, tile):
            col = lax.broadcasted_iota(jnp.int32, (1, tile), 1) + c
            zed = col >> 6
            col_id = col_base + (zed >> 3) * 4096 + (zed & 7) * 256 + (col & 63)
            square = lax.dot_general(
                rows[:, r : r + tile],
                columns[:, c : c + tile],
                (((0,), (0,)), ((), ())),
                preferred_element_type=F32,
            )
            guess = pl.reciprocal(square, approx=True)
            gain = guess * (2.0 - square * guess)
            if not far:
                gain = jnp.where(row_id == col_id, 0.0, gain)
            high, low = split(gain)
            highs.append(high)
            lows.append(low)
        gains = jnp.concatenate(highs + lows, axis=1)
        product = jnp.dot(gains, values, preferred_element_type=F32)
        part = product[:, :BANDS] + product[:, BANDS:]
        for ref in before:
            part = part + ref[r : r + tile, :]
        total_ref[r : r + tile, :] = part


def add_blocks(ref):
    total = ref[0]
    for k in range(1, NXY):
        total = total + ref[k]
    return total


def derive_kernel(parts_ref, powers_ref, sent_ref, user_ref, quality_ref, own_ref, column_ref):
    interference = add_blocks(parts_ref)
    lx, ly = user_ref[0:1, 0:BLOCK], user_ref[0:1, BLOCK:]
    dx = lx + 0.5 * sent_ref[BLOCK : BLOCK + 1, 0:BLOCK]
    dy = ly + 0.5 * sent_ref[BLOCK + 1 : BLOCK + 2, 0:BLOCK]
    own_gain = 1.0 / (1.0 + dx * dx + dy * dy)
    weight = WEIGHT_UNIT * user_ref[1:2, 0:BLOCK]
    fair = user_ref[1:2, BLOCK:]
    rows = jnp.concatenate([own_gain, weight, fair, jnp.zeros((5, BLOCK), F32)], axis=0)
    rows = jnp.concatenate([rows, jnp.zeros_like(rows)], axis=1)
    columns = jnp.concatenate([rows, jnp.zeros((120, 128), F32)], axis=0).T
    own_gain = columns[0:BLOCK, 0:1]
    weight = columns[0:BLOCK, 1:2]
    fair = columns[0:BLOCK, 2:3]
    signal = ARRAY_GAIN * own_gain * powers_ref[...]
    denominator = NOISE_POWER + interference
    quality = signal / denominator
    marginal = weight * jnp.exp(-fair * jnp.log(quality)) / denominator
    quality_ref[...] = quality
    own_ref[...] = ARRAY_GAIN * own_gain * marginal
    column_ref[0:BLOCK, :] = marginal * quality
    features = listener_features(lx.astype(jnp.int32), ly.astype(jnp.int32))
    column_ref[BLOCK:, :] = jnp.concatenate([features, jnp.zeros_like(features)], axis=1)


def finish_kernel(place_ref, parts_ref, own_ref, powers_ref, gradient_ref, power_ref, gap_ref):
    gradient = own_ref[...] - add_blocks(parts_ref)
    powers = powers_ref[...]
    target = PEAK_POWER * jax.nn.sigmoid(gradient)
    step_size = place_ref[7].astype(F32) / 4096.0
    gradient_ref[...] = gradient
    power_ref[...] = powers + step_size * (target - powers)
    gap = PEAK_POWER * jnp.maximum(gradient, 0.0) - gradient * powers
    gap = jnp.sum(gap, axis=0, keepdims=True)
    for k in range(NZ):
        gap_ref[k] = gap


def fold_kernel(parts_ref, out_ref):
    total = jnp.sum(parts_ref[...], axis=0)
    for k in range(2 * NXY):
        out_ref[k] = total


def last_kernel(parts_ref, late_ref, gap_ref, quality_ref):
    total = jnp.sum(jnp.sum(parts_ref[...], axis=0), axis=1, keepdims=True)
    gap_ref[...] = total / (USERS * BANDS)
    quality_ref[...] = late_ref[...]


def per_device(sender_xy, listener_xy, powers, weight, fairness, step_code):
    place = [lax.axis_index(name).astype(jnp.int32) for name in PLACE]
    place = jnp.stack([*place, step_code[0]])
    to_receiver = [((b % 32) * 16 + b // 32, b) for b in range(512)]
    swap = [(0, 1), (1, 0)]
    block, product = shape(BLOCK, BANDS), shape(ROWS, BANDS)
    work = dict(flops=2 * ROWS * HALF * 512, bytes_accessed=1 << 22)

    def gain_product(far, *args):
        def kernel(*refs):
            gain_kernel(far, *refs)

        return call(kernel, product, 1 + len(args), smem=(0,), **work)(place, *args)

    def spread_sum(near, far, plane):
        part = gain_product(False, plane, near)
        part = gain_product(True, plane, far, part)
        return lax.all_to_all(part.reshape(NXY, BLOCK, BANDS), XY, 0, 0)

    info = jnp.concatenate([sender_xy, listener_xy, weight[None], fairness[None]], axis=0)
    sent = call(pack_kernel, shape(SENT, BANDS), 2)(info, powers)
    near = lax.all_gather(sent, Z, axis=0)
    far = lax.ppermute(near, "core", swap)
    chunks = call(chunk_kernel, shape(NXY, 24, BANDS), 4, smem=(0,))(place, near, far, sent)
    chunks = lax.all_to_all(chunks, XY, 0, 0)
    features = shape(16, ROWS, dtype=BF16)
    listeners, senders, user = call(
        plane_kernel, (features, features, shape(8, BANDS)), 2, smem=(0,)
    )(place, chunks)
    parts = spread_sum(near, far, listeners)
    quality, own, column = call(derive_kernel, (block, block, shape(SENT, BANDS)), 4)(
        parts, powers, sent, user
    )

    near = lax.all_gather(column, Z, axis=0)
    far = lax.ppermute(near, "core", swap)
    parts = spread_sum(near, far, senders)
    gradient, new_power, gap = call(
        finish_kernel, (block, block, shape(NZ, 1, BANDS)), 4, smem=(0,)
    )(place, parts, own, powers)

    quality = lax.ppermute(quality, AXES, to_receiver)
    gap = lax.all_to_all(gap, Z, 0, 0)
    gap = call(fold_kernel, shape(2 * NXY, 1, BANDS), 1)(gap)
    gap = lax.all_to_all(gap, (*XY, "core"), 0, 0)
    gap, quality = call(last_kernel, (shape(1, 1), block), 2)(gap, quality)
    return quality, gradient, new_power, gap.reshape(1)


def solution(mesh):
    fine = Mesh(mesh.devices.reshape(SIZES), AXES)
    rx, tx = ("z2", "z1", "z0", "x"), ("y", "zhi", "core")
    by_sender, by_receiver = (*tx, *rx), (*rx, *tx)
    return jax.shard_map(
        per_device,
        mesh=fine,
        in_specs=(
            P(None, by_sender),
            P(None, by_receiver),
            P(by_sender, None),
            P(by_receiver),
            P(by_receiver),
            P(),
        ),
        out_specs=(P(by_receiver, None), P(by_sender, None), P(by_sender, None), P()),
        check_vma=False,
    )
```

```python
import jax
import jax.numpy as jnp
from jax import lax
from jax.experimental import pallas as pl
from jax.experimental.pallas import tpu as pltpu
from jax.sharding import Mesh
from jax.sharding import PartitionSpec as P

NOISE_POWER = 0.05
ARRAY_GAIN = 32.0
WEIGHT_UNIT = 1.0 / 16.0
PEAK_POWER = 1.0

AXES = ("z2", "z1", "z0", "x", "y", "zhi", "core")
SIZES = (2, 2, 2, 4, 4, 2, 2)
Z = ("zhi", "z2", "z1", "z0")
XY = ("x", "y")
PLACE = ("x", "y", "z0", "z2", "z1", "zhi", "core")
NZ, NXY = 16, 16
BLOCK, BANDS = 64, 128
SENT = BLOCK + 8
HALF = NZ * BLOCK
ROWS = NXY * BLOCK
USERS = 32768
VMEM_LIMIT = 20 * 1024 * 1024
F32, BF16 = jnp.float32, jnp.bfloat16


def whole():
    return pl.BlockSpec(memory_space=pltpu.VMEM)


def call(kernel, outs, n_in, flops=0, bytes_accessed=1 << 20, smem=()):
    def spec(i):
        return pl.BlockSpec(memory_space=pltpu.SMEM) if i in smem else whole()

    many = isinstance(outs, (list, tuple))
    return pl.pallas_call(
        kernel,
        out_shape=outs,
        in_specs=[spec(i) for i in range(n_in)],
        out_specs=[whole() for _ in outs] if many else whole(),
        compiler_params=pltpu.CompilerParams(vmem_limit_bytes=VMEM_LIMIT),
        cost_estimate=pl.CostEstimate(flops=flops, bytes_accessed=bytes_accessed, transcendentals=0),
    )


def shape(*dims, dtype=F32):
    return jax.ShapeDtypeStruct(dims, dtype)


def split_norm(norm):
    low = norm & 511
    odd = low & 1
    return norm - low, low - odd, odd


def listener_features(lx, ly):
    one = jnp.ones_like(lx)
    l1, l2, l3 = split_norm(lx * lx + ly * ly + 1)
    return jnp.concatenate([lx, ly, l1, l2, l3, one, one, one], axis=0).astype(F32)


def sender_features(sx, sy):
    one = jnp.ones_like(sx)
    s1, s2, s3 = split_norm(sx * sx + sy * sy)
    return jnp.concatenate([-2 * sx, -2 * sy, one, one, one, s1, s2, s3], axis=0).astype(F32)


def pack_kernel(info_ref, powers_ref, sent_ref):
    sent = sender_features(info_ref[0:1, :], info_ref[1:2, :])
    user = jnp.concatenate([info_ref[2:6, :].astype(F32), jnp.zeros((4, BLOCK), F32)], axis=0)
    sent_ref[0:BLOCK, :] = powers_ref[...]
    sent_ref[BLOCK:, :] = jnp.concatenate([sent, user], axis=1)


def chunk_kernel(place_ref, near_ref, far_ref, sent_ref, chunk_ref):
    zhi, core = place_ref[5], place_ref[6]
    users = []
    for k in range(NXY):
        there_x, there_y = k >> 2, k & 3
        at = (there_x >> 1) * 8 + there_y * 2 + zhi
        near, far = near_ref[at, BLOCK:, BLOCK:], far_ref[at, BLOCK:, BLOCK:]
        users.append(jnp.where(core == there_x & 1, near, far))
    places = [jnp.concatenate([user[0:1], user[1:2]], axis=1) for user in users]
    places = jnp.concatenate(places, axis=0)
    sender = -0.5 * sent_ref[BLOCK : BLOCK + 2, 0:BLOCK]
    sender = jnp.concatenate([sender[0:1], sender[1:2]], axis=1)
    for k, user in enumerate(users):
        weights = jnp.concatenate([user[2:3], user[3:4]], axis=1)
        tail = jnp.concatenate([sender, weights, jnp.zeros((6, BANDS), F32)], axis=0)
        chunk_ref[k, 0:NXY, :] = places
        chunk_ref[k, NXY:, :] = tail


def plane_kernel(place_ref, chunk_ref, listeners_ref, senders_ref, user_ref):
    x, y, z0, z2, z1, zhi, core = (place_ref[i] for i in range(7))
    source = (core * 2 + z2) * 4 + z1 * 2 + z0

    def line(pieces):
        pairs = [jnp.concatenate(pieces[k : k + 2], axis=1) for k in range(0, NXY, 2)]
        return jnp.concatenate(pairs, axis=1).astype(jnp.int32)

    def store(ref, features):
        ref[...] = jnp.concatenate([features, jnp.zeros_like(features)], axis=0).astype(BF16)

    left, right = slice(0, BLOCK), slice(BLOCK, 2 * BLOCK)
    places = chunk_ref[source, 0:NXY, :]
    lx, ly = (line([places[k : k + 1, half] for k in range(NXY)]) for half in (left, right))
    sx, sy = (line([chunk_ref[k, NXY : NXY + 1, half] for k in range(NXY)]) for half in (left, right))
    store(listeners_ref, listener_features(lx, ly))
    store(senders_ref, sender_features(sx, sy))
    user_ref[0:1, :] = chunk_ref[source, pl.ds(x * 4 + y, 1), :]
    user_ref[1:8, :] = chunk_ref[source, NXY + 1 :, :]


def spread(parts):
    pieces = []
    for k in range(0, 16, 2):
        left = parts[k, BLOCK:, 0:BLOCK]
        right = parts[k + 1, BLOCK:, 0:BLOCK]
        pieces.append(jnp.concatenate([left, right], axis=1))
    features = jnp.concatenate(pieces, axis=1)
    return jnp.concatenate([features, jnp.zeros_like(features)], axis=0).astype(BF16)


def split(value):
    high = value.astype(BF16)
    low = (value - high.astype(F32)).astype(BF16)
    return high, low


def gain_kernel(far, place_ref, plane_ref, column_ref, *rest):
    *before, total_ref = rest
    x, y, z0, z2, z1, zhi, core = (place_ref[i] for i in range(7))
    columns = spread(column_ref)
    value_high, value_low = split(column_ref[:, 0:BLOCK, :].reshape(HALF, BANDS))
    values = jnp.concatenate([value_high, value_low], axis=1)
    values = jnp.concatenate([values, values], axis=0)
    row_base = zhi * 4096 + core * 2048 + (z2 * 4 + z1 * 2 + z0) * 256
    col_base = y * 8192 + core * 2048 + x * 64
    tile = 128
    mine = (x * 4 + y) >> 1
    for turn in range(ROWS // tile):
        r = turn * tile if far else pl.multiple_of(((mine + turn) & 7) * tile, tile)
        row = lax.broadcasted_iota(jnp.int32, (tile, tile), 0) + r
        row_features = plane_ref[:, pl.ds(r, tile)]
        block = row >> 6
        row_id = row_base + (block & 3) * 8192 + (block >> 2) * 64 + (row & 63)
        highs, lows = [], []
        for c in range(0, HALF, tile):
            col = lax.broadcasted_iota(jnp.int32, (1, tile), 1) + c
            zed = col >> 6
            col_id = col_base + (zed >> 3) * 4096 + (zed & 7) * 256 + (col & 63)
            square = lax.dot_general(
                row_features,
                columns[:, c : c + tile],
                (((0,), (0,)), ((), ())),
                preferred_element_type=F32,
            )
            guess = pl.reciprocal(square, approx=True)
            gain = guess * (2.0 - square * guess)
            if not far and turn == 0:
                gain = jnp.where(row_id == col_id, 0.0, gain)
            high, low = split(gain)
            highs.append(high)
            lows.append(low)
        gains = jnp.concatenate(highs + lows, axis=1)
        product = jnp.dot(gains, values, preferred_element_type=F32)
        part = product[:, :BANDS] + product[:, BANDS:]
        for ref in before:
            part = part + ref[pl.ds(r, tile), :]
        total_ref[pl.ds(r, tile), :] = part


def add_blocks(ref):
    total = ref[0]
    for k in range(1, NXY):
        total = total + ref[k]
    return total


def derive_kernel(parts_ref, powers_ref, sent_ref, user_ref, quality_ref, own_ref, column_ref):
    interference = add_blocks(parts_ref)
    lx, ly = user_ref[0:1, 0:BLOCK], user_ref[0:1, BLOCK:]
    dx = lx + 0.5 * sent_ref[BLOCK : BLOCK + 1, 0:BLOCK]
    dy = ly + 0.5 * sent_ref[BLOCK + 1 : BLOCK + 2, 0:BLOCK]
    own_gain = 1.0 / (1.0 + dx * dx + dy * dy)
    weight = WEIGHT_UNIT * user_ref[1:2, 0:BLOCK]
    fair = user_ref[1:2, BLOCK:]
    rows = jnp.concatenate([own_gain, weight, fair, jnp.zeros((5, BLOCK), F32)], axis=0)
    rows = jnp.concatenate([rows, jnp.zeros_like(rows)], axis=1)
    columns = jnp.concatenate([rows, jnp.zeros((120, 128), F32)], axis=0).T
    own_gain = columns[0:BLOCK, 0:1]
    weight = columns[0:BLOCK, 1:2]
    fair = columns[0:BLOCK, 2:3]
    signal = ARRAY_GAIN * own_gain * powers_ref[...]
    denominator = NOISE_POWER + interference
    quality = signal / denominator
    marginal = weight * jnp.exp(-fair * jnp.log(quality)) / denominator
    quality_ref[...] = quality
    own_ref[...] = ARRAY_GAIN * own_gain * marginal
    column_ref[0:BLOCK, :] = marginal * quality
    features = listener_features(lx.astype(jnp.int32), ly.astype(jnp.int32))
    column_ref[BLOCK:, :] = jnp.concatenate([features, jnp.zeros_like(features)], axis=1)


def finish_kernel(place_ref, parts_ref, own_ref, powers_ref, gradient_ref, power_ref, gap_ref):
    gradient = own_ref[...] - add_blocks(parts_ref)
    powers = powers_ref[...]
    target = PEAK_POWER * jax.nn.sigmoid(gradient)
    step_size = place_ref[7].astype(F32) / 4096.0
    gradient_ref[...] = gradient
    power_ref[...] = powers + step_size * (target - powers)
    gap = PEAK_POWER * jnp.maximum(gradient, 0.0) - gradient * powers
    gap = jnp.sum(gap, axis=0, keepdims=True)
    for k in range(2 * NZ):
        gap_ref[k] = gap


def fold_kernel(parts_ref, out_ref):
    total = jnp.sum(parts_ref[...], axis=0)
    for k in range(NXY):
        out_ref[k] = total


def last_kernel(parts_ref, late_ref, gap_ref, quality_ref):
    total = jnp.sum(jnp.sum(parts_ref[...], axis=0), axis=1, keepdims=True)
    gap_ref[...] = total / (USERS * BANDS)
    quality_ref[...] = late_ref[...]


def per_device(sender_xy, listener_xy, powers, weight, fairness, step_code):
    place = [lax.axis_index(name).astype(jnp.int32) for name in PLACE]
    place = jnp.stack([*place, step_code[0]])
    to_receiver = [((b % 32) * 16 + b // 32, b) for b in range(512)]
    swap = [(0, 1), (1, 0)]
    block, product = shape(BLOCK, BANDS), shape(ROWS, BANDS)
    work = dict(flops=2 * ROWS * HALF * 512, bytes_accessed=1 << 22)

    def gain_product(far, *args):
        def kernel(*refs):
            gain_kernel(far, *refs)

        return call(kernel, product, 1 + len(args), smem=(0,), **work)(place, *args)

    def spread_sum(near, far, plane):
        part = gain_product(False, plane, near)
        part = gain_product(True, plane, far, part)
        return lax.all_to_all(part.reshape(NXY, BLOCK, BANDS), XY, 0, 0)

    info = jnp.concatenate([sender_xy, listener_xy, weight[None], fairness[None]], axis=0)
    sent = call(pack_kernel, shape(SENT, BANDS), 2)(info, powers)
    near = lax.all_gather(sent, Z, axis=0)
    far = lax.ppermute(near, "core", swap)
    chunks = call(chunk_kernel, shape(NXY, 24, BANDS), 4, smem=(0,))(place, near, far, sent)
    chunks = lax.all_to_all(chunks, XY, 0, 0)
    features = shape(16, ROWS, dtype=BF16)
    listeners, senders, user = call(
        plane_kernel, (features, features, shape(8, BANDS)), 2, smem=(0,)
    )(place, chunks)
    parts = spread_sum(near, far, listeners)
    quality, own, column = call(derive_kernel, (block, block, shape(SENT, BANDS)), 4)(
        parts, powers, sent, user
    )

    near = lax.all_gather(column, Z, axis=0)
    far = lax.ppermute(near, "core", swap)
    parts = spread_sum(near, far, senders)
    gradient, new_power, gap = call(
        finish_kernel, (block, block, shape(2 * NZ, 1, BANDS)), 4, smem=(0,)
    )(place, parts, own, powers)

    quality = lax.ppermute(quality, AXES, to_receiver)
    gap = lax.all_to_all(gap, (*Z, "core"), 0, 0)
    gap = call(fold_kernel, shape(NXY, 1, BANDS), 1)(gap)
    gap = lax.all_to_all(gap, XY, 0, 0)
    gap, quality = call(last_kernel, (shape(1, 1), block), 2)(gap, quality)
    return quality, gradient, new_power, gap.reshape(1)


def solution(mesh):
    fine = Mesh(mesh.devices.reshape(SIZES), AXES)
    rx, tx = ("z2", "z1", "z0", "x"), ("y", "zhi", "core")
    by_sender, by_receiver = (*tx, *rx), (*rx, *tx)
    return jax.shard_map(
        per_device,
        mesh=fine,
        in_specs=(
            P(None, by_sender),
            P(None, by_receiver),
            P(by_sender, None),
            P(by_receiver),
            P(by_receiver),
            P(),
        ),
        out_specs=(P(by_receiver, None), P(by_sender, None), P(by_sender, None), P()),
        check_vma=False,
    )
```

```python
import jax
import jax.numpy as jnp
from jax import lax
from jax.experimental import pallas as pl
from jax.experimental.pallas import tpu as pltpu
from jax.sharding import Mesh
from jax.sharding import PartitionSpec as P

NOISE_POWER = 0.05
ARRAY_GAIN = 32.0
WEIGHT_UNIT = 1.0 / 16.0
PEAK_POWER = 1.0

AXES = ("z2", "z1", "z0", "x", "y", "zhi", "core")
SIZES = (2, 2, 2, 4, 4, 2, 2)
Z = ("zhi", "z2", "z1", "z0")
XY = ("x", "y")
PLACE = ("x", "y", "z0", "z2", "z1", "zhi", "core")
NZ, NXY = 16, 16
BLOCK, BANDS = 64, 128
SENT = BLOCK + 8
HALF = NZ * BLOCK
ROWS = NXY * BLOCK
USERS = 32768
VMEM_LIMIT = 20 * 1024 * 1024
F32, BF16 = jnp.float32, jnp.bfloat16


def whole():
    return pl.BlockSpec(memory_space=pltpu.VMEM)


def call(kernel, outs, n_in, flops=0, bytes_accessed=1 << 20, smem=()):
    def spec(i):
        return pl.BlockSpec(memory_space=pltpu.SMEM) if i in smem else whole()

    many = isinstance(outs, (list, tuple))
    return pl.pallas_call(
        kernel,
        out_shape=outs,
        in_specs=[spec(i) for i in range(n_in)],
        out_specs=[whole() for _ in outs] if many else whole(),
        compiler_params=pltpu.CompilerParams(vmem_limit_bytes=VMEM_LIMIT),
        cost_estimate=pl.CostEstimate(flops=flops, bytes_accessed=bytes_accessed, transcendentals=0),
    )


def shape(*dims, dtype=F32):
    return jax.ShapeDtypeStruct(dims, dtype)


def split_norm(norm):
    low = norm & 511
    odd = low & 1
    return norm - low, low - odd, odd


def listener_features(lx, ly):
    one = jnp.ones_like(lx)
    l1, l2, l3 = split_norm(lx * lx + ly * ly + 1)
    return jnp.concatenate([lx, ly, l1, l2, l3, one, one, one], axis=0).astype(F32)


def sender_features(sx, sy):
    one = jnp.ones_like(sx)
    s1, s2, s3 = split_norm(sx * sx + sy * sy)
    return jnp.concatenate([-2 * sx, -2 * sy, one, one, one, s1, s2, s3], axis=0).astype(F32)


def pack_kernel(info_ref, powers_ref, sent_ref):
    sent = sender_features(info_ref[0:1, :], info_ref[1:2, :])
    user = jnp.concatenate([info_ref[2:6, :].astype(F32), jnp.zeros((4, BLOCK), F32)], axis=0)
    sent_ref[0:BLOCK, :] = powers_ref[...]
    sent_ref[BLOCK:, :] = jnp.concatenate([sent, user], axis=1)


def chunk_kernel(place_ref, near_ref, far_ref, sent_ref, chunk_ref):
    zhi, core = place_ref[5], place_ref[6]
    users = []
    for k in range(NXY):
        there_x, there_y = k >> 2, k & 3
        at = (there_x >> 1) * 8 + there_y * 2 + zhi
        near, far = near_ref[at, BLOCK:, BLOCK:], far_ref[at, BLOCK:, BLOCK:]
        users.append(jnp.where(core == there_x & 1, near, far))
    places = [jnp.concatenate([user[0:1], user[1:2]], axis=1) for user in users]
    places = jnp.concatenate(places, axis=0)
    sender = -0.5 * sent_ref[BLOCK : BLOCK + 2, 0:BLOCK]
    sender = jnp.concatenate([sender[0:1], sender[1:2]], axis=1)
    for k, user in enumerate(users):
        weights = jnp.concatenate([user[2:3], user[3:4]], axis=1)
        tail = jnp.concatenate([sender, weights, jnp.zeros((6, BANDS), F32)], axis=0)
        chunk_ref[k, 0:NXY, :] = places
        chunk_ref[k, NXY:, :] = tail


def plane_kernel(place_ref, chunk_ref, listeners_ref, senders_ref, user_ref):
    x, y, z0, z2, z1, zhi, core = (place_ref[i] for i in range(7))
    source = (core * 2 + z2) * 4 + z1 * 2 + z0

    def line(pieces):
        pairs = [jnp.concatenate(pieces[k : k + 2], axis=1) for k in range(0, NXY, 2)]
        return jnp.concatenate(pairs, axis=1).astype(jnp.int32)

    def store(ref, features):
        ref[...] = jnp.concatenate([features, jnp.zeros_like(features)], axis=0).astype(BF16)

    left, right = slice(0, BLOCK), slice(BLOCK, 2 * BLOCK)
    places = chunk_ref[source, 0:NXY, :]
    lx, ly = (line([places[k : k + 1, half] for k in range(NXY)]) for half in (left, right))
    sx, sy = (line([chunk_ref[k, NXY : NXY + 1, half] for k in range(NXY)]) for half in (left, right))
    store(listeners_ref, listener_features(lx, ly))
    store(senders_ref, sender_features(sx, sy))
    user_ref[0:1, :] = chunk_ref[source, pl.ds(x * 4 + y, 1), :]
    user_ref[1:8, :] = chunk_ref[source, NXY + 1 :, :]


def spread(parts):
    pieces = []
    for k in range(0, 16, 2):
        left = parts[k, BLOCK:, 0:BLOCK]
        right = parts[k + 1, BLOCK:, 0:BLOCK]
        pieces.append(jnp.concatenate([left, right], axis=1))
    features = jnp.concatenate(pieces, axis=1)
    return jnp.concatenate([features, jnp.zeros_like(features)], axis=0).astype(BF16)


def split(value):
    high = value.astype(BF16)
    low = (value - high.astype(F32)).astype(BF16)
    return high, low


def gain_kernel(far, place_ref, plane_ref, column_ref, *rest):
    *before, total_ref = rest
    x, y, z0, z2, z1, zhi, core = (place_ref[i] for i in range(7))
    columns = spread(column_ref)
    value_high, value_low = split(column_ref[:, 0:BLOCK, :].reshape(HALF, BANDS))
    values = jnp.concatenate([value_high, value_low], axis=1)
    row_base = zhi * 4096 + core * 2048 + (z2 * 4 + z1 * 2 + z0) * 256
    col_base = y * 8192 + core * 2048 + x * 64
    tile, wide = 128, 256
    mine = (x * 4 + y) >> 2
    for turn in range(ROWS // wide):
        r = turn * wide if far else pl.multiple_of(((mine + turn) & 3) * wide, wide)
        row = lax.broadcasted_iota(jnp.int32, (wide, tile), 0) + r
        row_features = plane_ref[:, pl.ds(r, wide)]
        block = row >> 6
        row_id = row_base + (block & 3) * 8192 + (block >> 2) * 64 + (row & 63)
        highs, lows = [], []
        for c in range(0, HALF, tile):
            col = lax.broadcasted_iota(jnp.int32, (1, tile), 1) + c
            zed = col >> 6
            col_id = col_base + (zed >> 3) * 4096 + (zed & 7) * 256 + (col & 63)
            square = lax.dot_general(
                row_features,
                columns[:, c : c + tile],
                (((0,), (0,)), ((), ())),
                preferred_element_type=F32,
            )
            guess = pl.reciprocal(square, approx=True)
            if not far and turn == 0:
                guess = jnp.where(row_id == col_id, 0.0, guess)
            high = guess.astype(BF16)
            highs.append(high)
            lows.append((guess * (1.0 - square * high.astype(F32))).astype(BF16))
        product = jnp.dot(jnp.concatenate(highs, axis=1), values, preferred_element_type=F32)
        part = product[:, :BANDS] + product[:, BANDS:]
        low_gain = jnp.concatenate(lows, axis=1)
        part = part + jnp.dot(low_gain, value_high, preferred_element_type=F32)
        for ref in before:
            part = part + ref[pl.ds(r, wide), :]
        total_ref[pl.ds(r, wide), :] = part


def add_blocks(ref):
    total = ref[0]
    for k in range(1, NXY):
        total = total + ref[k]
    return total


def derive_kernel(parts_ref, powers_ref, sent_ref, user_ref, quality_ref, own_ref, column_ref):
    interference = add_blocks(parts_ref)
    lx, ly = user_ref[0:1, 0:BLOCK], user_ref[0:1, BLOCK:]
    dx = lx + 0.5 * sent_ref[BLOCK : BLOCK + 1, 0:BLOCK]
    dy = ly + 0.5 * sent_ref[BLOCK + 1 : BLOCK + 2, 0:BLOCK]
    own_gain = 1.0 / (1.0 + dx * dx + dy * dy)
    weight = WEIGHT_UNIT * user_ref[1:2, 0:BLOCK]
    fair = user_ref[1:2, BLOCK:]
    rows = jnp.concatenate([own_gain, weight, fair, jnp.zeros((5, BLOCK), F32)], axis=0)
    rows = jnp.concatenate([rows, jnp.zeros_like(rows)], axis=1)
    columns = jnp.concatenate([rows, jnp.zeros((120, 128), F32)], axis=0).T
    own_gain = columns[0:BLOCK, 0:1]
    weight = columns[0:BLOCK, 1:2]
    fair = columns[0:BLOCK, 2:3]
    signal = ARRAY_GAIN * own_gain * powers_ref[...]
    denominator = NOISE_POWER + interference
    quality = signal / denominator
    marginal = weight * jnp.exp(-fair * jnp.log(quality)) / denominator
    quality_ref[...] = quality
    own_ref[...] = ARRAY_GAIN * own_gain * marginal
    column_ref[0:BLOCK, :] = marginal * quality
    features = listener_features(lx.astype(jnp.int32), ly.astype(jnp.int32))
    column_ref[BLOCK:, :] = jnp.concatenate([features, jnp.zeros_like(features)], axis=1)


def finish_kernel(place_ref, parts_ref, own_ref, powers_ref, gradient_ref, power_ref, gap_ref):
    gradient = own_ref[...] - add_blocks(parts_ref)
    powers = powers_ref[...]
    target = PEAK_POWER * jax.nn.sigmoid(gradient)
    step_size = place_ref[7].astype(F32) / 4096.0
    gradient_ref[...] = gradient
    power_ref[...] = powers + step_size * (target - powers)
    gap = PEAK_POWER * jnp.maximum(gradient, 0.0) - gradient * powers
    gap = jnp.sum(gap, axis=0, keepdims=True)
    for k in range(2 * NZ):
        gap_ref[k] = gap


def fold_kernel(parts_ref, out_ref):
    total = jnp.sum(parts_ref[...], axis=0)
    for k in range(NXY):
        out_ref[k] = total


def last_kernel(parts_ref, late_ref, gap_ref, quality_ref):
    total = jnp.sum(jnp.sum(parts_ref[...], axis=0), axis=1, keepdims=True)
    gap_ref[...] = total / (USERS * BANDS)
    quality_ref[...] = late_ref[...]


def per_device(sender_xy, listener_xy, powers, weight, fairness, step_code):
    place = [lax.axis_index(name).astype(jnp.int32) for name in PLACE]
    place = jnp.stack([*place, step_code[0]])
    to_receiver = [((b % 32) * 16 + b // 32, b) for b in range(512)]
    swap = [(0, 1), (1, 0)]
    block, product = shape(BLOCK, BANDS), shape(ROWS, BANDS)
    work = dict(flops=2 * ROWS * HALF * 512, bytes_accessed=1 << 22)

    def gain_product(far, *args):
        def kernel(*refs):
            gain_kernel(far, *refs)

        return call(kernel, product, 1 + len(args), smem=(0,), **work)(place, *args)

    def spread_sum(near, far, plane):
        part = gain_product(False, plane, near)
        part = gain_product(True, plane, far, part)
        return lax.all_to_all(part.reshape(NXY, BLOCK, BANDS), XY, 0, 0)

    info = jnp.concatenate([sender_xy, listener_xy, weight[None], fairness[None]], axis=0)
    sent = call(pack_kernel, shape(SENT, BANDS), 2)(info, powers)
    near = lax.all_gather(sent, Z, axis=0)
    far = lax.ppermute(near, "core", swap)
    chunks = call(chunk_kernel, shape(NXY, 24, BANDS), 4, smem=(0,))(place, near, far, sent)
    chunks = lax.all_to_all(chunks, XY, 0, 0)
    features = shape(16, ROWS, dtype=BF16)
    listeners, senders, user = call(
        plane_kernel, (features, features, shape(8, BANDS)), 2, smem=(0,)
    )(place, chunks)
    parts = spread_sum(near, far, listeners)
    quality, own, column = call(derive_kernel, (block, block, shape(SENT, BANDS)), 4)(
        parts, powers, sent, user
    )

    near = lax.all_gather(column, Z, axis=0)
    far = lax.ppermute(near, "core", swap)
    parts = spread_sum(near, far, senders)
    gradient, new_power, gap = call(
        finish_kernel, (block, block, shape(2 * NZ, 1, BANDS)), 4, smem=(0,)
    )(place, parts, own, powers)

    quality = lax.ppermute(quality, AXES, to_receiver)
    gap = lax.all_to_all(gap, (*Z, "core"), 0, 0)
    gap = call(fold_kernel, shape(NXY, 1, BANDS), 1)(gap)
    gap = lax.all_to_all(gap, XY, 0, 0)
    gap, quality = call(last_kernel, (shape(1, 1), block), 2)(gap, quality)
    return quality, gradient, new_power, gap.reshape(1)


def solution(mesh):
    fine = Mesh(mesh.devices.reshape(SIZES), AXES)
    rx, tx = ("z2", "z1", "z0", "x"), ("y", "zhi", "core")
    by_sender, by_receiver = (*tx, *rx), (*rx, *tx)
    return jax.shard_map(
        per_device,
        mesh=fine,
        in_specs=(
            P(None, by_sender),
            P(None, by_receiver),
            P(by_sender, None),
            P(by_receiver),
            P(by_receiver),
            P(),
        ),
        out_specs=(P(by_receiver, None), P(by_sender, None), P(by_sender, None), P()),
        check_vma=False,
    )
```
